32 devices in a mesh: row: 16 (over z, x, core), col: 2 (over y).
Axes of the slice: x: 2, y: 2, z: 4, core: 2. Of those that a mesh axis runs over, the one named last changes fastest.
Arguments:
- amplitudes: bfloat16 [128, 64, 256], P('col', 'row'), may hold values from -6 to 6
- integrals: bfloat16 [64, 12, 256, 256], P('row', 'col'), may hold values from -0.0625 to 0.0625
- screen: int32 [64, 12], P('row', 'col'), may hold values from -1 to 7, as said below
- owner_map: int32 [2, 8], P('col'), may hold values from 0 to 7, each once within a row
Outputs:
- ladder: float32 [128, 16, 256], P('row', 'col')
The draws below stay inside these ranges and needn't reach their ends.
Inputs may be any that keep to these rules, and one draw needn't show every extreme that they name: `screen`: in each row and column group the 6 slots first name distinct result tiles of that group, then hold -1; at least 2 are live, and some group of some row has all 6 live.
All inputs are finite; a program needn't handle non-finite values.
Results may differ from the reference program's by a relative error of at most 0.0003.
Values may be sent and summed in bfloat16 or wider, within the bound.
No kernel may reach another device: no remote copies, remote signals or barrier semaphores. Data moves between devices by JAX's collectives and lax.ppermute only.
A program may use at most 64 MiB of HBM per device.

```python
import jax
import jax.numpy as jnp
from jax import lax

TILE = 256
SLOTS = 6
AB_COL = 8
PAIRS = 128
NCD = 64
NAB = 16
LISTS = 12
N_COL = 2


def draw_screen(key, part):
    count_rows = NCD * N_COL
    keys = jax.random.split(jax.random.fold_in(key, 11), count_rows)
    perms = jax.vmap(lambda single: jax.random.permutation(single, AB_COL))(keys)[:, :SLOTS]
    counts = jax.random.randint(jax.random.fold_in(key, 12), (count_rows,), 2, SLOTS + 1)
    counts = counts.at[0].set(SLOTS)
    position = jnp.arange(SLOTS, dtype=jnp.int32)
    lists = jnp.where(position[None, :] < counts[:, None], perms.astype(jnp.int32), -1)
    return lists.reshape(NCD, N_COL * SLOTS).astype(jnp.int32)


def steps_of(own_key, shape, shards, low, largest):
    gain, own = 1.0, jax.random.fold_in(own_key, 6)
    for axis_at, blocks in shards:
        draws = jnp.exp(jax.random.uniform(jax.random.fold_in(own, axis_at), (blocks,), jnp.float32, low / len(shards), largest / len(shards)))
        gain = gain * jnp.repeat(draws, shape[axis_at] // blocks).reshape([-1 if axis == axis_at else 1 for axis in range(len(shape))])
    return gain


def scatter_about(stream_key, dims, width, most, cuts=(), kind=jnp.bfloat16):
    array = jax.random.normal(stream_key, dims, jnp.float32) * width
    if len(cuts) > 0:
        array = steps_of(stream_key, dims, cuts, -0.22, 0.18) * array
    return jnp.clip(array, min=-most, max=most).astype(kind)


def setup_inputs(seed: int = 0) -> dict:
    seeds = jax.random.split(jax.random.key(seed), 5)
    amplitudes = scatter_about(seeds[0], (PAIRS, NCD, TILE), 1.0, 6.0, ((0, 2), (1, 16)))
    integrals = scatter_about(seeds[1], (NCD, LISTS, TILE, TILE), (NCD * TILE // 2) ** -0.5, 0.0625, ((0, 16), (1, 2)))
    screen = draw_screen(jax.random.fold_in(seeds[4], 71), 0)
    owner_map = jax.vmap(lambda own: jax.random.permutation(own, AB_COL))(jax.random.split(seeds[3], N_COL)).reshape((N_COL, AB_COL)).astype(jnp.int32)
    return {"amplitudes": amplitudes, "integrals": integrals, "screen": screen, "owner_map": owner_map}


def reference(amplitudes, integrals, screen, owner_map):
    lists = screen.reshape(NCD, N_COL, SLOTS)
    live = lists >= 0
    safe = jnp.maximum(lists, 0)
    table = jnp.broadcast_to(owner_map[None, :, :], (NCD, N_COL, AB_COL))
    stored = jnp.take_along_axis(table, safe, axis=2)
    groups = jnp.arange(N_COL, dtype=jnp.int32)[None, :, None] * AB_COL
    target = (stored + groups).reshape(NCD, LISTS)
    livemask = live.reshape(NCD, LISTS)
    columns = jnp.arange(NAB, dtype=jnp.int32)
    onehot = ((target[:, :, None] == columns[None, None, :]) & livemask[:, :, None]).astype(jnp.float32)

    def step(total, index):
        amp_tile = lax.dynamic_index_in_dim(amplitudes, index, 1, keepdims=False).astype(jnp.float32)
        blocks = lax.dynamic_index_in_dim(integrals, index, 0, keepdims=False).astype(jnp.float32)
        select = lax.dynamic_index_in_dim(onehot, index, 0, keepdims=False)
        contrib = jnp.einsum('pw,swv->psv', amp_tile, blocks, precision=lax.Precision.HIGHEST)
        total = total + jnp.einsum('psv,sa->pav', contrib, select, precision=lax.Precision.HIGHEST)
        return total, None

    start = jnp.zeros((PAIRS, NAB, TILE), jnp.float32)
    result, unused = lax.scan(step, start, jnp.arange(NCD, dtype=jnp.int32))
    return result
```

```python
import functools

import jax
import jax.numpy as jnp
from jax import lax
from jax.experimental import pallas as pl
from jax.experimental.pallas import tpu as pltpu
from jax.sharding import PartitionSpec as P

def partial_kernel(n_col, masks, size, screen, owner, own, *refs):
    others, integrals = refs[: n_col - 1], refs[n_col - 1]
    send, keep = refs[n_col], refs[n_col + 1 : -3]
    lhs, total, table = refs[-3:]
    tiles, slots = screen.shape
    targets = owner.shape[1]
    half = own.shape[1]
    row, col = lax.axis_index("row"), lax.axis_index("col")

    for at in range(tiles * targets):
        table[at] = -1
    for k in range(tiles):
        for s in range(slots):
            name = screen[k, s]
            stored = owner[0, jnp.maximum(name, 0)]
            table[jnp.where(name >= 0, k * targets + stored, tiles * targets)] = s

    for step in range(n_col):
        source = own if step == 0 else others[step - 1]
        owner_col = lax.rem(col + n_col - step, n_col)
        for k in range(tiles):
            lhs[k, pl.ds(pl.multiple_of(owner_col * half, half), half), :] = source[k]

    for t in range(targets):
        acc = None
        for k in range(tiles):
            s = table[k * targets + t]
            left = jnp.where(s >= 0, lhs[k], jnp.zeros_like(lhs[k]))
            term = jnp.dot(left, integrals[k, jnp.maximum(s, 0)], preferred_element_type=jnp.float32)
            acc = term if acc is None else acc + term
        total[t] = acc

    def block(t, j):
        return total[t, pl.ds(pl.multiple_of((row ^ j) * size, size), size), :]

    order = [0]
    for m in reversed(masks):
        order = order + [m ^ o for o in order]
    parts, low = [], 0
    for ref in reversed(keep):
        parts.append((ref, order[low : low + ref.shape[0]]))
        low += ref.shape[0]
    for t in range(targets):
        rows = pl.ds(t * size, size)
        for at, j in enumerate(order):
            send[at, rows, :] = block(t, j ^ 1)
        for ref, js in parts:
            for at, j in enumerate(js):
                ref[at, rows, :] = block(t, j)


def final_kernel(targets, size, a, b, out):
    x = a[0] + b[0]
    for t in range(targets):
        out[:, t, :] = x[t * size : (t + 1) * size, :]


def body(n_row, n_col, amplitudes, integrals, screen, owner_map):
    half, tiles, width = amplitudes.shape
    targets = owner_map.shape[1]
    out_width = integrals.shape[3]
    depth = n_row.bit_length() - 1
    masks = [1 << b for b in range(1, depth)]
    pairs = half * n_col
    size = pairs // n_row

    def vmem(x):
        return pltpu.with_memory_space_constraint(x, pltpu.VMEM)

    def swap(x, mask):
        return lax.ppermute(x, "row", [(i, i ^ mask) for i in range(n_row)])

    own = jnp.transpose(amplitudes, (1, 0, 2))
    others = [
        lax.ppermute(own, "col", [(i, (i + step) % n_col) for i in range(n_col)])
        for step in range(1, n_col)
    ]
    sizes = [1 << (len(masks) - 1 - i) for i in range(len(masks))] + [1]
    block = (targets * size, out_width)
    spec = pl.BlockSpec(memory_space=pltpu.VMEM)
    smem = pl.BlockSpec(memory_space=pltpu.SMEM)
    outs = pl.pallas_call(
        functools.partial(partial_kernel, n_col, masks, size),
        out_shape=[pltpu.VMEM((n_row // 2,) + block, jnp.float32)]
        + [pltpu.VMEM((n,) + block, jnp.float32) for n in sizes],
        in_specs=[smem, smem] + [spec] * (n_col + 1),
        out_specs=[spec] * (1 + len(sizes)),
        scratch_shapes=[
            pltpu.VMEM((tiles, pairs, width), jnp.bfloat16),
            pltpu.VMEM((targets, pairs, out_width), jnp.float32),
            pltpu.SMEM((tiles * targets + 1,), jnp.int32),
        ],
        cost_estimate=pl.CostEstimate(
            flops=2 * pairs * tiles * targets * width * out_width,
            bytes_accessed=integrals.size * 2,
            transcendentals=0,
        ),
        compiler_params=pltpu.CompilerParams(vmem_limit_bytes=24 * 1024 * 1024),
        name="partial_sums",
    )(screen, owner_map, vmem(own), *[vmem(o) for o in others], vmem(integrals))
    send, keep = outs[0], list(outs[1:])

    got = swap(send, 1)
    for at, mask in enumerate([None] + masks[:-1]):
        if mask is not None:
            got = swap(keep[0], mask)
            keep = keep[1:]
        top = got.shape[0]
        fresh = []
        for part in keep:
            fresh.append(part + got[top - part.shape[0] : top])
            top -= part.shape[0]
        keep = fresh
    got = swap(keep[0], masks[-1])
    return pl.pallas_call(
        functools.partial(final_kernel, targets, size),
        out_shape=jax.ShapeDtypeStruct((size, targets, out_width), jnp.float32),
        in_specs=[spec, spec],
        out_specs=spec,
        name="own_block",
    )(vmem(keep[1]), vmem(got))


def solution(mesh):
    return jax.shard_map(
        functools.partial(body, mesh.shape["row"], mesh.shape["col"]),
        mesh=mesh,
        in_specs=(
            P("col", "row", None),
            P("row", "col", None, None),
            P("row", "col"),
            P("col", None),
        ),
        out_specs=P("row", "col", None),
        check_vma=False,
    )
```

```python
import functools

import jax
import jax.numpy as jnp
from jax import lax
from jax.experimental import pallas as pl
from jax.experimental.pallas import tpu as pltpu
from jax.sharding import PartitionSpec as P

def place_kernel(screen_hbm, owner_hbm, own_hbm, integrals, placed, own, screen, owner, table, raw, sems, small):
    tiles, slots = screen.shape
    targets = owner.shape[1]
    loads = [
        pltpu.make_async_copy(src, dst, small.at[at])
        for at, (src, dst) in enumerate(((screen_hbm, screen), (owner_hbm, owner), (own_hbm, raw)))
    ]
    for load in loads:
        load.start()
    for at in range(tiles * targets):
        table[at] = 0
    for load in loads[:2]:
        load.wait()

    def live_copy(k, s):
        name = screen[k, s]
        t = owner[0, jnp.maximum(name, 0)]
        copy = pltpu.make_async_copy(integrals.at[k, s], placed.at[t, k], sems.at[k, s])
        return name >= 0, t, copy

    for k in range(tiles):
        for s in range(slots):
            live, t, copy = live_copy(k, s)

            @pl.when(live)
            def _():
                copy.start()
                table[k * targets + t] = 1

    loads[2].wait()
    own[...] = jnp.swapaxes(raw[...], 0, 1)
    for k in range(tiles):
        for t in range(targets):

            @pl.when(table[k * targets + t] == 0)
            def _():
                placed[t, k] = jnp.zeros(placed.shape[2:], placed.dtype)

    for k in range(tiles):
        for s in range(slots):
            live, t, copy = live_copy(k, s)

            @pl.when(live)
            def _():
                copy.wait()


def partial_kernel(n_col, masks, size, own, *refs):
    others, placed = refs[: n_col - 1], refs[n_col - 1]
    send, keep = refs[n_col], refs[n_col + 1 : -2]
    lhs, total = refs[-2:]
    tiles, half, width = own.shape
    targets = placed.shape[0]
    row, col = lax.axis_index("row"), lax.axis_index("col")

    for step in range(n_col):
        source = own[...] if step == 0 else jnp.swapaxes(others[step - 1][...], 0, 1)
        owner_col = lax.rem(col + n_col - step, n_col)
        for k in range(tiles):
            lhs[pl.ds(pl.multiple_of(owner_col * half, half), half), k * width : (k + 1) * width] = source[k]

    for t in range(targets):
        weights = placed[t].reshape(tiles * width, placed.shape[3])
        total[t] = jnp.dot(lhs[...], weights, preferred_element_type=jnp.float32)

    def block(t, j):
        return total[t, pl.ds(pl.multiple_of((row ^ j) * size, size), size), :]

    order = [0]
    for m in reversed(masks):
        order = order + [m ^ o for o in order]
    parts, low = [], 0
    for ref in reversed(keep):
        parts.append((ref, order[low : low + ref.shape[0]]))
        low += ref.shape[0]
    for t in range(targets):
        rows = pl.ds(t * size, size)
        for at, j in enumerate(order):
            send[at, rows, :] = block(t, j ^ 1)
        for ref, js in parts:
            for at, j in enumerate(js):
                ref[at, rows, :] = block(t, j)


def final_kernel(targets, size, a, b, out):
    x = a[0] + b[0]
    for t in range(targets):
        out[:, t, :] = x[t * size : (t + 1) * size, :]


def body(n_row, n_col, amplitudes, integrals, screen, owner_map):
    half, tiles, width = amplitudes.shape
    targets = owner_map.shape[1]
    out_width = integrals.shape[3]
    depth = n_row.bit_length() - 1
    masks = [1 << b for b in range(1, depth)]
    pairs = half * n_col
    size = pairs // n_row

    def vmem(x):
        return pltpu.with_memory_space_constraint(x, pltpu.VMEM)

    def swap(x, mask):
        return lax.ppermute(x, "row", [(i, i ^ mask) for i in range(n_row)])

    others = [
        lax.ppermute(amplitudes, "col", [(i, (i + step) % n_col) for i in range(n_col)])
        for step in range(1, n_col)
    ]
    sizes = [1 << (len(masks) - 1 - i) for i in range(len(masks))] + [1]
    block = (targets * size, out_width)
    spec = pl.BlockSpec(memory_space=pltpu.VMEM)
    hbm = pl.BlockSpec(memory_space=pl.ANY)
    params = pltpu.CompilerParams(vmem_limit_bytes=24 * 1024 * 1024)
    placed, own = pl.pallas_call(
        place_kernel,
        out_shape=[
            pltpu.VMEM((targets, tiles, width, out_width), jnp.bfloat16),
            pltpu.VMEM((tiles, half, width), jnp.bfloat16),
        ],
        in_specs=[hbm] * 4,
        out_specs=[spec, spec],
        scratch_shapes=[
            pltpu.SMEM(screen.shape, jnp.int32),
            pltpu.SMEM(owner_map.shape, jnp.int32),
            pltpu.SMEM((tiles * targets,), jnp.int32),
            pltpu.VMEM(amplitudes.shape, jnp.bfloat16),
            pltpu.SemaphoreType.DMA(screen.shape),
            pltpu.SemaphoreType.DMA((3,)),
        ],
        cost_estimate=pl.CostEstimate(flops=0, bytes_accessed=integrals.size * 2, transcendentals=0),
        compiler_params=params,
        name="place_tiles",
    )(*[pltpu.with_memory_space_constraint(x, pltpu.HBM) for x in (screen, owner_map, amplitudes, integrals)])
    outs = pl.pallas_call(
        functools.partial(partial_kernel, n_col, masks, size),
        out_shape=[pltpu.VMEM((n_row // 2,) + block, jnp.float32)]
        + [pltpu.VMEM((n,) + block, jnp.float32) for n in sizes],
        in_specs=[spec] * (n_col + 1),
        out_specs=[spec] * (1 + len(sizes)),
        scratch_shapes=[
            pltpu.VMEM((pairs, tiles * width), jnp.bfloat16),
            pltpu.VMEM((targets, pairs, out_width), jnp.float32),
        ],
        cost_estimate=pl.CostEstimate(
            flops=2 * pairs * tiles * targets * width * out_width, bytes_accessed=0, transcendentals=0
        ),
        compiler_params=params,
        name="partial_sums",
    )(vmem(own), *[vmem(o) for o in others], vmem(placed))
    send, keep = outs[0], list(outs[1:])

    got = swap(send, 1)
    for at, mask in enumerate([None] + masks[:-1]):
        if mask is not None:
            got = swap(keep[0], mask)
            keep = keep[1:]
        top = got.shape[0]
        fresh = []
        for part in keep:
            fresh.append(part + got[top - part.shape[0] : top])
            top -= part.shape[0]
        keep = fresh
    got = swap(keep[0], masks[-1])
    return pl.pallas_call(
        functools.partial(final_kernel, targets, size),
        out_shape=jax.ShapeDtypeStruct((size, targets, out_width), jnp.float32),
        in_specs=[spec, spec],
        out_specs=spec,
        name="own_block",
    )(vmem(keep[1]), vmem(got))


def solution(mesh):
    return jax.shard_map(
        functools.partial(body, mesh.shape["row"], mesh.shape["col"]),
        mesh=mesh,
        in_specs=(
            P("col", "row", None),
            P("row", "col", None, None),
            P("row", "col"),
            P("col", None),
        ),
        out_specs=P("row", "col", None),
        check_vma=False,
    )
```

```python
import functools

import jax
import jax.numpy as jnp
from jax import lax
from jax.experimental import pallas as pl
from jax.experimental.pallas import tpu as pltpu
from jax.sharding import PartitionSpec as P

SPARE = 16
LEAST = -100

def place_kernel(screen_hbm, owner_hbm, own_hbm, integrals, placed, own, screen, owner, table, raw, sems, small):
    tiles, slots = screen.shape
    targets = owner.shape[1]
    loads = [
        pltpu.make_async_copy(src, dst, small.at[at])
        for at, (src, dst) in enumerate(((screen_hbm, screen), (owner_hbm, owner), (own_hbm, raw)))
    ]
    for load in loads:
        load.start()
    for at in range(tiles * targets):
        table[at] = 0
    for load in loads[:2]:
        load.wait()

    def live_copy(k, s):
        name = screen[k, s]
        t = owner[0, jnp.maximum(name, 0)]
        copy = pltpu.make_async_copy(integrals.at[k, s], placed.at[t, k], sems.at[k, s])
        return name >= 0, t, copy

    for k in range(tiles):
        for s in range(slots):
            live, t, copy = live_copy(k, s)

            @pl.when(live)
            def _():
                copy.start()
                table[k * targets + t] = 1

    loads[2].wait()
    own[...] = jnp.swapaxes(raw[...], 0, 1)
    for k in range(tiles):
        for t in range(targets):

            @pl.when(table[k * targets + t] == 0)
            def _():
                placed[t, k] = jnp.zeros(placed.shape[2:], placed.dtype)

    for k in range(tiles):
        for s in range(slots):
            live, t, copy = live_copy(k, s)

            @pl.when(live)
            def _():
                copy.wait()


def partial_kernel(n_col, order, size, own, *refs):
    others, placed = refs[: n_col - 1], refs[n_col - 1]
    send, keep, lhs, total = refs[n_col:]
    tiles, half, width = own.shape
    targets = placed.shape[0]
    row, col = lax.axis_index("row"), lax.axis_index("col")

    for step in range(n_col):
        source = own[...] if step == 0 else jnp.swapaxes(others[step - 1][...], 0, 1)
        owner_col = lax.rem(col + n_col - step, n_col)
        for k in range(tiles):
            lhs[pl.ds(pl.multiple_of(owner_col * half, half), half), k * width : (k + 1) * width] = source[k]

    for t in range(targets):
        weights = placed[t].reshape(tiles * width, placed.shape[3])
        total[t] = jnp.dot(lhs[...], weights, preferred_element_type=jnp.float32)

    def block(t, j):
        return total[t, pl.ds(pl.multiple_of((row ^ j) * size, size), size), :]

    for t in range(targets):
        rows = pl.ds(t * size, size)
        for at, j in enumerate(order):
            send[at, rows, :] = block(t, j ^ 1)
            keep[at, rows, :] = block(t, j)


def encode(values, out):
    rows, width = values[0].shape
    at_row = lax.broadcasted_iota(jnp.int32, (SPARE, width), 0)
    exponents = jnp.zeros((SPARE, width), jnp.int32)
    for at, x in enumerate(values):
        largest = jnp.maximum(jnp.max(jnp.abs(x), axis=0, keepdims=True), 2.0**LEAST)
        exponent = jnp.floor(jnp.log2(largest)) + 1.0
        code = jnp.round(x * jnp.exp2(15.0 - exponent))
        code = jnp.clip(code, -32767.0, 32767.0).astype(jnp.int32)
        out[at * rows : (at + 1) * rows, :] = code.astype(jnp.int16)
        exponents = jnp.where(at_row == at, exponent.astype(jnp.int32), exponents)
    out[len(values) * rows :, :] = exponents.astype(jnp.int16)


def decode(coded, at, rows):
    count = (coded.shape[0] - SPARE) // rows
    exponents = coded[count * rows :, :].astype(jnp.int32)[at : at + 1, :].astype(jnp.float32)
    code = coded[at * rows : (at + 1) * rows, :].astype(jnp.int32).astype(jnp.float32)
    return code * jnp.exp2(exponents - 15.0)


def first_kernel(groups, keep, got, *outs):
    at = 0
    for out, count in zip(outs, groups):
        values = [keep[at + i] + got[at + i] for i in range(count)]
        if out is outs[-1]:
            for i in range(count):
                out[i] = values[i]
        else:
            encode(values, out)
        at += count


def next_kernel(groups, arrived, keep, *refs):
    coded, outs = refs[:arrived], refs[arrived:]
    at = 0
    for out, count in zip(outs, groups):
        values = []
        for i in range(at, at + count):
            x = keep[i]
            for part in coded:
                x = x + decode(part, i, keep.shape[1])
            values.append(x)
        if out is outs[-1]:
            for i in range(count):
                out[i] = values[i]
        else:
            encode(values, out)
        at += count


def final_kernel(targets, size, keep, *refs):
    coded, out = refs[:-1], refs[-1]
    x = keep[0]
    for part in coded:
        x = x + decode(part, 0, targets * size)
    for t in range(targets):
        out[:, t, :] = x[t * size : (t + 1) * size, :]


def body(n_row, n_col, amplitudes, integrals, screen, owner_map):
    half, tiles, width = amplitudes.shape
    targets = owner_map.shape[1]
    out_width = integrals.shape[3]
    depth = n_row.bit_length() - 1
    masks = [1 << b for b in range(1, depth)]
    pairs = half * n_col
    size = pairs // n_row

    def vmem(x):
        return pltpu.with_memory_space_constraint(x, pltpu.VMEM)

    def swap(x, mask):
        return lax.ppermute(x, "row", [(i, i ^ mask) for i in range(n_row)])

    others = [
        lax.ppermute(amplitudes, "col", [(i, (i + step) % n_col) for i in range(n_col)])
        for step in range(1, n_col)
    ]
    stages = [masks[at : at + 2] for at in range(0, len(masks), 2)]
    plans, order = [], [0]
    for stage in reversed(stages):
        partners = [0]
        for mask in stage:
            partners = [mask | p for p in partners] + partners
        plans.insert(0, (partners[:-1], len(order)))
        order = [p ^ o for p in partners for o in order]
    block = (targets * size, out_width)
    spec = pl.BlockSpec(memory_space=pltpu.VMEM)
    hbm = pl.BlockSpec(memory_space=pl.ANY)
    params = pltpu.CompilerParams(vmem_limit_bytes=24 * 1024 * 1024)
    placed, own = pl.pallas_call(
        place_kernel,
        out_shape=[
            pltpu.VMEM((targets, tiles, width, out_width), jnp.bfloat16),
            pltpu.VMEM((tiles, half, width), jnp.bfloat16),
        ],
        in_specs=[hbm] * 4,
        out_specs=[spec, spec],
        scratch_shapes=[
            pltpu.SMEM(screen.shape, jnp.int32),
            pltpu.SMEM(owner_map.shape, jnp.int32),
            pltpu.SMEM((tiles * targets,), jnp.int32),
            pltpu.VMEM(amplitudes.shape, jnp.bfloat16),
            pltpu.SemaphoreType.DMA(screen.shape),
            pltpu.SemaphoreType.DMA((3,)),
        ],
        cost_estimate=pl.CostEstimate(flops=0, bytes_accessed=integrals.size * 2, transcendentals=0),
        compiler_params=params,
        name="place_tiles",
    )(*[pltpu.with_memory_space_constraint(x, pltpu.HBM) for x in (screen, owner_map, amplitudes, integrals)])
    outs = pl.pallas_call(
        functools.partial(partial_kernel, n_col, order, size),
        out_shape=[pltpu.VMEM((len(order),) + block, jnp.float32)] * 2,
        in_specs=[spec] * (n_col + 1),
        out_specs=[spec] * 2,
        scratch_shapes=[
            pltpu.VMEM((pairs, tiles * width), jnp.bfloat16),
            pltpu.VMEM((targets, pairs, out_width), jnp.float32),
        ],
        cost_estimate=pl.CostEstimate(
            flops=2 * pairs * tiles * targets * width * out_width, bytes_accessed=0, transcendentals=0
        ),
        compiler_params=params,
        name="partial_sums",
    )(vmem(own), *[vmem(o) for o in others], vmem(placed))
    send, keep = outs
    arrived = [swap(send, 1)]
    for at, (partners, count) in enumerate(plans):
        groups = [count] * (len(partners) + 1)
        step = (
            functools.partial(first_kernel, groups)
            if at == 0
            else functools.partial(next_kernel, groups, len(arrived))
        )
        *coded, keep = pl.pallas_call(
            step,
            out_shape=[pltpu.VMEM((count * block[0] + SPARE, out_width), jnp.int16)] * len(partners)
            + [pltpu.VMEM((count,) + block, jnp.float32)],
            in_specs=[spec] * (1 + len(arrived)),
            out_specs=[spec] * (1 + len(partners)),
            compiler_params=params,
            name="encode_stage",
        )(vmem(keep), *[vmem(part) for part in arrived])
        arrived = [swap(part, partner) for part, partner in zip(coded, partners)]
    return pl.pallas_call(
        functools.partial(final_kernel, targets, size),
        out_shape=jax.ShapeDtypeStruct((size, targets, out_width), jnp.float32),
        in_specs=[spec] * (1 + len(arrived)),
        out_specs=spec,
        compiler_params=params,
        name="own_block",
    )(vmem(keep), *[vmem(part) for part in arrived])


def solution(mesh):
    return jax.shard_map(
        functools.partial(body, mesh.shape["row"], mesh.shape["col"]),
        mesh=mesh,
        in_specs=(
            P("col", "row", None),
            P("row", "col", None, None),
            P("row", "col"),
            P("col", None),
        ),
        out_specs=P("row", "col", None),
        check_vma=False,
    )
```

```python
import functools

import jax
import jax.numpy as jnp
from jax import lax
from jax.experimental import pallas as pl
from jax.experimental.pallas import tpu as pltpu
from jax.sharding import PartitionSpec as P

SPARE = 16
LEAST = -100
LANES = 128
ACROSS, ALONG = 2, 4


def place(size, total, places):
    targets, near = total.shape[0] - 1, total.shape[1] // size
    low = lax.rem(lax.axis_index("row"), near)
    for ref, at, offset in places:
        first = pl.multiple_of((low ^ offset) * size, size)
        for t in range(targets):
            ref[at, t * size : (t + 1) * size, :] = total[t, pl.ds(first, size), :]


def lay_out(size, totals, keep, send):
    second = lax.rem(lax.axis_index("row"), 2) == 1
    mine, other = jnp.where(second, ALONG, ACROSS), jnp.where(second, ACROSS, ALONG)
    for h, total in enumerate(totals):
        kept = (ACROSS | ALONG, mine, mine ^ 1, 0)
        sent = (ACROSS | ALONG | 1, other ^ 1, other, 1)
        places = [(keep, 4 * h + at, j) for at, j in enumerate(kept)]
        place(size, total, places + [(send, 4 * h + at, j) for at, j in enumerate(sent)])


def sides(raw):
    by_tile = jnp.swapaxes(raw, 0, 1)
    return [by_tile[k] for k in range(by_tile.shape[0])]


def spare(count):
    return -(-count // SPARE) * SPARE


def encode(values, out):
    rows, width = values[0].shape
    pieces = [x[:, c : c + LANES] for x in values for c in range(0, width, LANES)]
    last = spare(len(pieces))
    at_row = lax.broadcasted_iota(jnp.int32, (last, LANES), 0)
    exponents = jnp.zeros((last, LANES), jnp.int32)
    for at, x in enumerate(pieces):
        largest = jnp.maximum(jnp.max(jnp.abs(x), axis=0, keepdims=True), 2.0**LEAST)
        exponent = jnp.floor(jnp.log2(largest)) + 1.0
        code = jnp.round(x * jnp.exp2(15.0 - exponent))
        code = jnp.clip(code, -32767.0, 32767.0).astype(jnp.int32)
        out[at * rows : (at + 1) * rows, :] = code.astype(jnp.int16)
        exponents = jnp.where(at_row == at, exponent.astype(jnp.int32), exponents)
    data = len(pieces) * rows
    for at in range(data, out.shape[0] - last, SPARE):
        out[at : at + SPARE, :] = jnp.zeros((SPARE, LANES), jnp.int16)
    out[out.shape[0] - last :, :] = exponents.astype(jnp.int16)


def decode(coded, at, rows, width):
    each = width // LANES
    count = coded.shape[0] // rows
    exponents = coded[coded.shape[0] - spare(count) :, :].astype(jnp.int32)
    parts = []
    for i in range(at * each, (at + 1) * each):
        code = coded[i * rows : (i + 1) * rows, :].astype(jnp.int32).astype(jnp.float32)
        parts.append(code * jnp.exp2(exponents[i : i + 1, :].astype(jnp.float32) - 15.0))
    return jnp.concatenate(parts, axis=1)


def early_kernel(
    size, screen_hbm, owner_hbm, own_hbm, integrals,
    tiles, aim, send, keep, screen, owner, raw, total, sems, small,
):
    depth, slots = screen.shape
    targets = owner.shape[1]
    loads = [
        pltpu.make_async_copy(src, dst, small.at[at])
        for at, (src, dst) in enumerate(((screen_hbm, screen), (owner_hbm, owner), (own_hbm, raw)))
    ]

    for load in loads:
        load.start()
    copies = [
        pltpu.make_async_copy(integrals.at[k], tiles.at[pl.ds(k * slots, slots)], sems.at[k]) for k in range(depth)
    ]
    for at, copy in enumerate(copies):
        copy.start(priority=min(at, 1))
    total[...] = jnp.zeros(total.shape, total.dtype)
    for load in loads:
        load.wait()
    for k in range(depth):
        for s in range(slots):
            name = screen[k, s]
            aim[k * slots + s] = jnp.where(name >= 0, owner[0, jnp.maximum(name, 0)], targets)
    lhs = sides(raw[...])
    for k in range(depth):
        copies[k].wait()
        for s in range(slots):
            add_tile(lhs[k], tiles, aim, k * slots + s, total)
    lay_out(size, [total], keep, send)


def add_tile(lhs, tiles, aim, i, total):
    t = aim[i]
    total[t] += jnp.dot(lhs, tiles[i], preferred_element_type=jnp.float32)


def late_kernel(size, count, *refs):
    others, (tiles, aim, out, keep, send, totals) = refs[:count], refs[count:]
    slots = aim.shape[0] // others[0].shape[1]
    totals[...] = jnp.zeros(totals.shape, totals.dtype)
    for h, raw in enumerate(others):
        lhs = sides(raw[...])
        for i in range(aim.shape[0]):
            add_tile(lhs[i // slots], tiles, aim, i, totals.at[h])
    lay_out(size, [totals.at[h] for h in range(count)], keep, send)
    encode([send[i] for i in range(4 * count)], out)


def early_sums_kernel(keep, got, ahead, out):
    sums = [keep[at] + got[at] for at in range(4)]
    encode(sums[1:3], ahead)
    out[0] = sums[0]
    out[1] = sums[3]


def near_kernel(n_col, early, late_keep, late_got, side, diagonal, out):
    rows, width = early.shape[1:]
    sums = []
    for at in range(4):
        sums.append([late_keep[i] + decode(late_got, i, rows, width) for i in range(at, (n_col - 1) * 4, 4)])
    encode(sums[1] + sums[2], side)
    encode([early[0]] + sums[0], diagonal)
    out[0] = early[1]
    for h in range(n_col - 1):
        out[1 + h] = sums[3][h]


def emit(groups, values, outs):
    at = 0
    for out, count in zip(outs, groups):
        if out is outs[-1]:
            for i in range(count):
                out[i] = values[at + i]
        else:
            encode(values[at : at + count], out)
        at += count


def pass_kernel(rows, each, ahead, side, out):
    late = (side.shape[0] // rows) // 2
    out[:rows, :] = ahead[rows : 2 * rows, :]
    out[rows : (1 + late) * rows, :] = side[late * rows : 2 * late * rows, :]
    first = ahead[ahead.shape[0] - SPARE :, :].astype(jnp.int32)[each : 2 * each]
    rest = side[2 * late * rows :, :].astype(jnp.int32)[late * each : 2 * late * each]
    last = out.shape[0] - (1 + late) * rows
    lines = [first, rest]
    if last > (1 + late) * each:
        lines.append(jnp.zeros((last - (1 + late) * each, LANES), jnp.int32))
    out[(1 + late) * rows :, :] = jnp.concatenate(lines, axis=0).astype(jnp.int16)


def sort_kernel(n_col, near, far, groups, keep, ahead, side, diagonal, passed, *refs):
    outs, sums = refs[:-1], refs[-1]
    rows, width = keep.shape[1:]
    for h in range(n_col):
        x = keep[h] + (decode(ahead, 0, rows, width) if h == 0 else decode(side, h - 1, rows, width))
        x = x + decode(passed, h, rows, width)
        sums[h] = x + decode(diagonal, h, rows, width)
    high, col = lax.axis_index("row") // near, lax.axis_index("col")
    emit(groups, [sums[lax.rem(col + n_col - (high ^ j), n_col)] for j in far], outs)


def far_kernel(groups, arrived, keep, *refs):
    coded, outs = refs[:arrived], refs[arrived:]
    rows, width = keep.shape[1:]
    values = []
    for i in range(sum(groups)):
        x = keep[i]
        for part in coded:
            x = x + decode(part, i, rows, width)
        values.append(x)
    emit(groups, values, outs)


def last_kernel(targets, size, keep, *refs):
    coded, out = refs[:-1], refs[-1]
    x = keep[0]
    for part in coded:
        x = x + decode(part, 0, targets * size, x.shape[1])
    for t in range(targets):
        out[:, t, :] = x[t * size : (t + 1) * size, :]


def offsets(masks):
    order = [0]
    for mask in masks:
        order = [mask | o for o in order] + order
    return order


def body(n_row, n_col, amplitudes, integrals, screen, owner_map):
    half, depth, width = amplitudes.shape
    slots, targets, out_width = integrals.shape[1], owner_map.shape[1], integrals.shape[3]
    size = half * n_col // n_row
    near = n_row // n_col
    spec = pl.BlockSpec(memory_space=pltpu.VMEM)
    smem = pl.BlockSpec(memory_space=pltpu.SMEM)
    hbm = pl.BlockSpec(memory_space=pltpu.HBM)
    params = pltpu.CompilerParams(vmem_limit_bytes=24 * 1024 * 1024)
    block = (targets * size, out_width)

    def vmem(x):
        return pltpu.with_memory_space_constraint(x, pltpu.VMEM)

    def swap(x, mask):
        return lax.ppermute(x, "row", [(i, i ^ mask) for i in range(n_row)])

    def call(kernel, name, out_shape, *operands, **more):
        single = not isinstance(out_shape, list)
        return pl.pallas_call(
            kernel,
            out_shape=out_shape,
            in_specs=[spec] * len(operands),
            out_specs=spec if single else [spec] * len(out_shape),
            compiler_params=params,
            name=name,
            **more,
        )(*[vmem(x) for x in operands])

    def coded(count, more=0):
        count *= out_width // LANES
        return pltpu.VMEM((count * block[0] + more + spare(count), LANES), jnp.int16)

    def kept(count):
        return pltpu.VMEM((count,) + block, jnp.float32)

    others = [
        lax.ppermute(amplitudes, "col", [(i, (i + step) % n_col) for i in range(n_col)])
        for step in range(1, n_col)
    ]
    half_cost = pl.CostEstimate(
        flops=2 * half * depth * targets * width * out_width, bytes_accessed=0, transcendentals=0
    )
    tiles, aim, send, keep = pl.pallas_call(
        functools.partial(early_kernel, size),
        out_shape=[
            pltpu.VMEM((depth * slots, width, out_width), jnp.bfloat16),
            pltpu.SMEM((depth * slots,), jnp.int32),
            kept(4),
            kept(4),
        ],
        in_specs=[hbm] * 4,
        out_specs=[spec, smem, spec, spec],
        scratch_shapes=[
            pltpu.SMEM(screen.shape, jnp.int32),
            pltpu.SMEM(owner_map.shape, jnp.int32),
            pltpu.VMEM(amplitudes.shape, jnp.bfloat16),
            pltpu.VMEM((targets + 1, half, out_width), jnp.float32),
            pltpu.SemaphoreType.DMA((depth,)),
            pltpu.SemaphoreType.DMA((3,)),
        ],
        cost_estimate=pl.CostEstimate(
            flops=half_cost.flops, bytes_accessed=integrals.size * 2, transcendentals=0
        ),
        compiler_params=params,
        name="early_half",
    )(*[pltpu.with_memory_space_constraint(x, pltpu.HBM) for x in (screen, owner_map, amplitudes, integrals)])
    got = swap(send, 1)

    lates = n_col - 1
    late_send, late_keep = pl.pallas_call(
        functools.partial(late_kernel, size, lates),
        out_shape=[coded(lates * 4), kept(lates * 4)],
        in_specs=[spec] * n_col + [smem],
        out_specs=[spec, spec],
        scratch_shapes=[
            pltpu.VMEM((lates * 4,) + block, jnp.float32),
            pltpu.VMEM((lates, targets + 1, half, out_width), jnp.float32),
        ],
        cost_estimate=half_cost,
        compiler_params=params,
        name="late_half",
    )(*[vmem(o) for o in others], vmem(tiles), pltpu.with_memory_space_constraint(aim, pltpu.SMEM))
    late_got = swap(late_send, 1)
    def to_side(x):
        return lax.ppermute(x, "row", [(i, i ^ (ALONG if i % 2 else ACROSS)) for i in range(n_row)])

    ahead, early = call(early_sums_kernel, "early_sums", [coded(2, SPARE), kept(2)], keep, got)
    ahead = to_side(ahead)
    side, diagonal, keep = call(
        functools.partial(near_kernel, n_col),
        "near_sums",
        [coded(2 * lates), coded(n_col), kept(n_col)],
        early,
        late_keep,
        late_got,
    )
    side = to_side(side)
    diagonal = swap(diagonal, ACROSS | ALONG)
    each = out_width // LANES
    passed = call(functools.partial(pass_kernel, each * block[0], each), "pass_on", coded(n_col), ahead, side)
    arrived = [ahead, side, diagonal, swap(passed, 1)]

    masks = [near << b for b in range(n_col.bit_length() - 1)]
    plans, far = [], [0]
    for stage in reversed([masks[at : at + 2] for at in range(0, len(masks), 2)]):
        partners = offsets(stage)
        plans.insert(0, (partners, len(far)))
        far = [p | o for p in partners for o in far]
    for at, (partners, count) in enumerate(plans):
        groups = [count] * len(partners)
        if at == 0:
            offs = [o // near for o in far]
            kernel = functools.partial(sort_kernel, n_col, near, offs, groups)
            more = dict(scratch_shapes=[pltpu.VMEM((n_col,) + block, jnp.float32)])
        else:
            kernel, more = functools.partial(far_kernel, groups, len(arrived)), {}
        *parts, keep = call(
            kernel, "far_sums", [coded(count)] * (len(partners) - 1) + [kept(count)], keep, *arrived, **more
        )
        arrived = [swap(part, partner) for part, partner in zip(parts, partners)]
    return pl.pallas_call(
        functools.partial(last_kernel, targets, size),
        out_shape=jax.ShapeDtypeStruct((size, targets, out_width), jnp.float32),
        in_specs=[spec] * (1 + len(arrived)),
        out_specs=spec,
        compiler_params=params,
        name="own_block",
    )(vmem(keep), *[vmem(part) for part in arrived])


def solution(mesh):
    return jax.shard_map(
        functools.partial(body, mesh.shape["row"], mesh.shape["col"]),
        mesh=mesh,
        in_specs=(
            P("col", "row", None),
            P("row", "col", None, None),
            P("row", "col"),
            P("col", None),
        ),
        out_specs=P("row", "col", None),
        check_vma=False,
    )
```

```python
import functools

import jax
import jax.numpy as jnp
from jax import lax
from jax.experimental import pallas as pl
from jax.experimental.pallas import tpu as pltpu
from jax.sharding import PartitionSpec as P

SPARE = 16
LEAST = -100
LANES = 128
ACROSS, ALONG = 2, 4


def place(size, total, places):
    targets, near = total.shape[0] - 1, total.shape[1] // size
    low = lax.rem(lax.axis_index("row"), near)
    for ref, at, offset in places:
        first = pl.multiple_of((low ^ offset) * size, size)
        for t in range(targets):
            ref[at, t * size : (t + 1) * size, :] = total[t, pl.ds(first, size), :]


def pairs_of(masks):
    return [masks[at : at + 2] for at in range(0, len(masks), 2)]


def lay_out(size, n_col, step, totals, keep, send):
    row, col = lax.axis_index("row"), lax.axis_index("col")
    second = lax.rem(row, 2) == 1
    mine, other = jnp.where(second, ALONG, ACROSS), jnp.where(second, ACROSS, ALONG)
    near = totals[0].shape[1] // size
    for h, total in enumerate(totals):
        offset = (row // near) ^ lax.rem(col + n_col - step - h, n_col)
        flip = 0
        for stage in pairs_of([1 << b for b in range(n_col.bit_length() - 1)]):
            flip = flip ^ jnp.where(offset & sum(stage) != 0, 1, 0)
        kept = (ACROSS | ALONG, mine, mine ^ 1, 0)
        sent = (ACROSS | ALONG | 1, other ^ 1, other, 1)
        places = [(keep, 4 * h + at, j ^ flip) for at, j in enumerate(kept)]
        place(size, total, places + [(send, 4 * h + at, j ^ flip) for at, j in enumerate(sent)])


def sides(raw):
    by_tile = jnp.swapaxes(raw, 0, 1)
    return [by_tile[k] for k in range(by_tile.shape[0])]


def spare(count):
    return -(-count // SPARE) * SPARE


def encode(values, out):
    rows, width = values[0].shape
    pieces = [x[:, c : c + LANES] for x in values for c in range(0, width, LANES)]
    last = spare(len(pieces))
    at_row = lax.broadcasted_iota(jnp.int32, (last, LANES), 0)
    exponents = jnp.zeros((last, LANES), jnp.int32)
    for at, x in enumerate(pieces):
        largest = jnp.maximum(jnp.max(jnp.abs(x), axis=0, keepdims=True), 2.0**LEAST)
        exponent = jnp.floor(jnp.log2(largest)) + 1.0
        code = jnp.round(x * jnp.exp2(15.0 - exponent))
        code = jnp.clip(code, -32767.0, 32767.0).astype(jnp.int32)
        out[at * rows : (at + 1) * rows, :] = code.astype(jnp.int16)
        exponents = jnp.where(at_row == at, exponent.astype(jnp.int32), exponents)
    data = len(pieces) * rows
    for at in range(data, out.shape[0] - last, SPARE):
        out[at : at + SPARE, :] = jnp.zeros((SPARE, LANES), jnp.int16)
    out[out.shape[0] - last :, :] = exponents.astype(jnp.int16)


def decode(coded, at, rows, width):
    each = width // LANES
    count = coded.shape[0] // rows
    exponents = coded[coded.shape[0] - spare(count) :, :].astype(jnp.int32)
    parts = []
    for i in range(at * each, (at + 1) * each):
        code = coded[i * rows : (i + 1) * rows, :].astype(jnp.int32).astype(jnp.float32)
        parts.append(code * jnp.exp2(exponents[i : i + 1, :].astype(jnp.float32) - 15.0))
    return jnp.concatenate(parts, axis=1)


def early_kernel(
    size, n_col, screen_hbm, owner_hbm, own_hbm, integrals,
    tiles, aim, send, keep, screen, owner, raw, total, sems, small,
):
    depth, slots = screen.shape
    targets = owner.shape[1]
    loads = [
        pltpu.make_async_copy(src, dst, small.at[at])
        for at, (src, dst) in enumerate(((screen_hbm, screen), (owner_hbm, owner), (own_hbm, raw)))
    ]

    for load in loads:
        load.start()
    copies = [
        pltpu.make_async_copy(integrals.at[k], tiles.at[pl.ds(k * slots, slots)], sems.at[k]) for k in range(depth)
    ]
    for at, copy in enumerate(copies):
        copy.start(priority=min(at, 1))
    total[...] = jnp.zeros(total.shape, total.dtype)
    for load in loads:
        load.wait()
    for k in range(depth):
        for s in range(slots):
            name = screen[k, s]
            aim[k * slots + s] = jnp.where(name >= 0, owner[0, jnp.maximum(name, 0)], targets)
    lhs = sides(raw[...])
    for k in range(depth):
        copies[k].wait()
        for s in range(slots):
            add_tile(lhs[k], tiles, aim, k * slots + s, total)
    lay_out(size, n_col, 0, [total], keep, send)


def add_tile(lhs, tiles, aim, i, total):
    t = aim[i]
    total[t] += jnp.dot(lhs, tiles[i], preferred_element_type=jnp.float32)


def late_kernel(size, count, *refs):
    others, (tiles, aim, out, keep, send, totals) = refs[:count], refs[count:]
    slots = aim.shape[0] // others[0].shape[1]
    totals[...] = jnp.zeros(totals.shape, totals.dtype)
    for h, raw in enumerate(others):
        lhs = sides(raw[...])
        for i in range(aim.shape[0]):
            add_tile(lhs[i // slots], tiles, aim, i, totals.at[h])
    lay_out(size, count + 1, 1, [totals.at[h] for h in range(count)], keep, send)
    encode([send[i] for i in range(4 * count)], out)


def early_sums_kernel(keep, got, ahead, out):
    sums = [keep[at] + got[at] for at in range(4)]
    encode(sums[1:3], ahead)
    out[0] = sums[0]
    out[1] = sums[3]


def near_kernel(n_col, early, late_keep, late_got, side, diagonal, out):
    rows, width = early.shape[1:]
    sums = []
    for at in range(4):
        sums.append([late_keep[i] + decode(late_got, i, rows, width) for i in range(at, (n_col - 1) * 4, 4)])
    encode(sums[1] + sums[2], side)
    encode([early[0]] + sums[0], diagonal)
    out[0] = early[1]
    for h in range(n_col - 1):
        out[1 + h] = sums[3][h]


def emit(groups, values, outs):
    at = 0
    for out, count in zip(outs, groups):
        if out is outs[-1]:
            for i in range(count):
                out[i] = values[at + i]
        else:
            encode(values[at : at + count], out)
        at += count


def pass_kernel(rows, each, ahead, side, out):
    late = (side.shape[0] // rows) // 2
    out[:rows, :] = ahead[rows : 2 * rows, :]
    out[rows : (1 + late) * rows, :] = side[late * rows : 2 * late * rows, :]
    first = ahead[ahead.shape[0] - SPARE :, :].astype(jnp.int32)[each : 2 * each]
    rest = side[2 * late * rows :, :].astype(jnp.int32)[late * each : 2 * late * each]
    last = out.shape[0] - (1 + late) * rows
    lines = [first, rest]
    if last > (1 + late) * each:
        lines.append(jnp.zeros((last - (1 + late) * each, LANES), jnp.int32))
    out[(1 + late) * rows :, :] = jnp.concatenate(lines, axis=0).astype(jnp.int16)


def sort_kernel(n_col, near, far, groups, keep, ahead, side, diagonal, passed, *refs):
    outs, sums = refs[:-1], refs[-1]
    rows, width = keep.shape[1:]
    for h in range(n_col):
        x = keep[h] + (decode(ahead, 0, rows, width) if h == 0 else decode(side, h - 1, rows, width))
        x = x + decode(passed, h, rows, width)
        sums[h] = x + decode(diagonal, h, rows, width)
    high, col = lax.axis_index("row") // near, lax.axis_index("col")
    emit(groups, [sums[lax.rem(col + n_col - (high ^ j), n_col)] for j in far], outs)


def far_kernel(groups, arrived, keep, *refs):
    coded, outs = refs[:arrived], refs[arrived:]
    rows, width = keep.shape[1:]
    values = []
    for i in range(sum(groups)):
        x = keep[i]
        for part in coded:
            x = x + decode(part, i, rows, width)
        values.append(x)
    emit(groups, values, outs)


def last_kernel(targets, size, keep, *refs):
    coded, out = refs[:-1], refs[-1]
    x = keep[0]
    for part in coded:
        x = x + decode(part, 0, targets * size, x.shape[1])
    for t in range(targets):
        out[:, t, :] = x[t * size : (t + 1) * size, :]


def offsets(masks):
    order = [0]
    for mask in masks:
        order = [mask | o for o in order] + order
    return order


def body(n_row, n_col, amplitudes, integrals, screen, owner_map):
    half, depth, width = amplitudes.shape
    slots, targets, out_width = integrals.shape[1], owner_map.shape[1], integrals.shape[3]
    size = half * n_col // n_row
    near = n_row // n_col
    spec = pl.BlockSpec(memory_space=pltpu.VMEM)
    smem = pl.BlockSpec(memory_space=pltpu.SMEM)
    hbm = pl.BlockSpec(memory_space=pltpu.HBM)
    params = pltpu.CompilerParams(vmem_limit_bytes=24 * 1024 * 1024)
    block = (targets * size, out_width)

    def vmem(x):
        return pltpu.with_memory_space_constraint(x, pltpu.VMEM)

    def swap(x, mask):
        return lax.ppermute(x, "row", [(i, i ^ mask) for i in range(n_row)])

    def call(kernel, name, out_shape, *operands, **more):
        single = not isinstance(out_shape, list)
        return pl.pallas_call(
            kernel,
            out_shape=out_shape,
            in_specs=[spec] * len(operands),
            out_specs=spec if single else [spec] * len(out_shape),
            compiler_params=params,
            name=name,
            **more,
        )(*[vmem(x) for x in operands])

    def coded(count, more=0):
        count *= out_width // LANES
        return pltpu.VMEM((count * block[0] + more + spare(count), LANES), jnp.int16)

    def kept(count):
        return pltpu.VMEM((count,) + block, jnp.float32)

    others = [
        lax.ppermute(amplitudes, "col", [(i, (i + step) % n_col) for i in range(n_col)])
        for step in range(1, n_col)
    ]
    half_cost = pl.CostEstimate(
        flops=2 * half * depth * targets * width * out_width, bytes_accessed=0, transcendentals=0
    )
    tiles, aim, send, keep = pl.pallas_call(
        functools.partial(early_kernel, size, n_col),
        out_shape=[
            pltpu.VMEM((depth * slots, width, out_width), jnp.bfloat16),
            pltpu.SMEM((depth * slots,), jnp.int32),
            kept(4),
            kept(4),
        ],
        in_specs=[hbm] * 4,
        out_specs=[spec, smem, spec, spec],
        scratch_shapes=[
            pltpu.SMEM(screen.shape, jnp.int32),
            pltpu.SMEM(owner_map.shape, jnp.int32),
            pltpu.VMEM(amplitudes.shape, jnp.bfloat16),
            pltpu.VMEM((targets + 1, half, out_width), jnp.float32),
            pltpu.SemaphoreType.DMA((depth,)),
            pltpu.SemaphoreType.DMA((3,)),
        ],
        cost_estimate=pl.CostEstimate(
            flops=half_cost.flops, bytes_accessed=integrals.size * 2, transcendentals=0
        ),
        compiler_params=params,
        name="early_half",
    )(*[pltpu.with_memory_space_constraint(x, pltpu.HBM) for x in (screen, owner_map, amplitudes, integrals)])
    got = swap(send, 1)

    lates = n_col - 1
    late_send, late_keep = pl.pallas_call(
        functools.partial(late_kernel, size, lates),
        out_shape=[coded(lates * 4), kept(lates * 4)],
        in_specs=[spec] * n_col + [smem],
        out_specs=[spec, spec],
        scratch_shapes=[
            pltpu.VMEM((lates * 4,) + block, jnp.float32),
            pltpu.VMEM((lates, targets + 1, half, out_width), jnp.float32),
        ],
        cost_estimate=half_cost,
        compiler_params=params,
        name="late_half",
    )(*[vmem(o) for o in others], vmem(tiles), pltpu.with_memory_space_constraint(aim, pltpu.SMEM))
    late_got = swap(late_send, 1)
    def to_side(x):
        return lax.ppermute(x, "row", [(i, i ^ (ALONG if i % 2 else ACROSS)) for i in range(n_row)])

    ahead, early = call(early_sums_kernel, "early_sums", [coded(2, SPARE), kept(2)], keep, got)
    ahead = to_side(ahead)
    side, diagonal, keep = call(
        functools.partial(near_kernel, n_col),
        "near_sums",
        [coded(2 * lates), coded(n_col), kept(n_col)],
        early,
        late_keep,
        late_got,
    )
    side = to_side(side)
    diagonal = swap(diagonal, ACROSS | ALONG)
    each = out_width // LANES
    passed = call(functools.partial(pass_kernel, each * block[0], each), "pass_on", coded(n_col), ahead, side)
    arrived = [ahead, side, diagonal, swap(passed, 1)]

    masks = [near << b for b in range(n_col.bit_length() - 1)]
    plans, far = [], [0]
    for stage in reversed(pairs_of(masks)):
        partners = offsets(stage)
        plans.insert(0, (partners, len(far)))
        far = [p | o for p in partners for o in far]
    for at, (partners, count) in enumerate(plans):
        groups = [count] * len(partners)
        if at == 0:
            offs = [o // near for o in far]
            kernel = functools.partial(sort_kernel, n_col, near, offs, groups)
            more = dict(scratch_shapes=[pltpu.VMEM((n_col,) + block, jnp.float32)])
        else:
            kernel, more = functools.partial(far_kernel, groups, len(arrived)), {}
        *parts, keep = call(
            kernel, "far_sums", [coded(count)] * (len(partners) - 1) + [kept(count)], keep, *arrived, **more
        )
        arrived = [swap(part, partner | 1) for part, partner in zip(parts, partners)]
    return pl.pallas_call(
        functools.partial(last_kernel, targets, size),
        out_shape=jax.ShapeDtypeStruct((size, targets, out_width), jnp.float32),
        in_specs=[spec] * (1 + len(arrived)),
        out_specs=spec,
        compiler_params=params,
        name="own_block",
    )(vmem(keep), *[vmem(part) for part in arrived])


def solution(mesh):
    return jax.shard_map(
        functools.partial(body, mesh.shape["row"], mesh.shape["col"]),
        mesh=mesh,
        in_specs=(
            P("col", "row", None),
            P("row", "col", None, None),
            P("row", "col"),
            P("col", None),
        ),
        out_specs=P("row", "col", None),
        check_vma=False,
    )
```

```python
import functools

import jax
import jax.numpy as jnp
from jax import lax
from jax.experimental import pallas as pl
from jax.experimental.pallas import tpu as pltpu
from jax.sharding import PartitionSpec as P

SPARE = 16
LEAST = -100
LANES = 128
ACROSS, ALONG = 2, 4


def place(size, total, places):
    targets, near = total.shape[0] - 1, total.shape[1] // size
    low = lax.rem(lax.axis_index("row"), near)
    for ref, at, offset in places:
        first = pl.multiple_of((low ^ offset) * size, size)
        for t in range(targets):
            ref[at, t * size : (t + 1) * size, :] = total[t, pl.ds(first, size), :]


def pairs_of(masks):
    return [masks[at : at + 2] for at in range(0, len(masks), 2)]


def lay_out(size, n_col, step, totals, keep, send):
    row, col = lax.axis_index("row"), lax.axis_index("col")
    second = lax.rem(row, 2) == 1
    mine, other = jnp.where(second, ALONG, ACROSS), jnp.where(second, ACROSS, ALONG)
    near = totals[0].shape[1] // size
    for h, total in enumerate(totals):
        offset = (row // near) ^ lax.rem(col + n_col - step - h, n_col)
        flip = 0
        for stage in pairs_of([1 << b for b in range(n_col.bit_length() - 1)]):
            flip = flip ^ jnp.where(offset & sum(stage) != 0, 1, 0)
        kept = (ACROSS | ALONG | 1, mine ^ 1, mine, 0)
        sent = (ACROSS | ALONG, other, other ^ 1, 1)
        places = [(keep, 4 * h + at, j ^ flip) for at, j in enumerate(kept)]
        place(size, total, places + [(send, 4 * h + at, j ^ flip) for at, j in enumerate(sent)])


def sides(raw):
    by_tile = jnp.swapaxes(raw, 0, 1)
    return [by_tile[k] for k in range(by_tile.shape[0])]


def spare(count):
    return -(-count // SPARE) * SPARE


def encode(values, out):
    rows, width = values[0].shape
    pieces = [x[:, c : c + LANES] for x in values for c in range(0, width, LANES)]
    last = spare(len(pieces))
    at_row = lax.broadcasted_iota(jnp.int32, (last, LANES), 0)
    exponents = jnp.zeros((last, LANES), jnp.int32)
    for at, x in enumerate(pieces):
        largest = jnp.maximum(jnp.max(jnp.abs(x), axis=0, keepdims=True), 2.0**LEAST)
        exponent = jnp.floor(jnp.log2(largest)) + 1.0
        code = jnp.round(x * jnp.exp2(15.0 - exponent))
        code = jnp.clip(code, -32767.0, 32767.0).astype(jnp.int32)
        out[at * rows : (at + 1) * rows, :] = code.astype(jnp.int16)
        exponents = jnp.where(at_row == at, exponent.astype(jnp.int32), exponents)
    data = len(pieces) * rows
    for at in range(data, out.shape[0] - last, SPARE):
        out[at : at + SPARE, :] = jnp.zeros((SPARE, LANES), jnp.int16)
    out[out.shape[0] - last :, :] = exponents.astype(jnp.int16)


def decode(coded, at, rows, width):
    each = width // LANES
    count = coded.shape[0] // rows
    exponents = coded[coded.shape[0] - spare(count) :, :].astype(jnp.int32)
    parts = []
    for i in range(at * each, (at + 1) * each):
        code = coded[i * rows : (i + 1) * rows, :].astype(jnp.int32).astype(jnp.float32)
        parts.append(code * jnp.exp2(exponents[i : i + 1, :].astype(jnp.float32) - 15.0))
    return jnp.concatenate(parts, axis=1)


def early_kernel(
    size, n_col, screen_hbm, owner_hbm, own_hbm, integrals,
    tiles, aim, send, keep, screen, owner, raw, total, sems, small,
):
    depth, slots = screen.shape
    targets = owner.shape[1]
    loads = [
        pltpu.make_async_copy(src, dst, small.at[at])
        for at, (src, dst) in enumerate(((screen_hbm, screen), (owner_hbm, owner), (own_hbm, raw)))
    ]

    for load in loads:
        load.start()
    copies = [
        pltpu.make_async_copy(integrals.at[k], tiles.at[pl.ds(k * slots, slots)], sems.at[k]) for k in range(depth)
    ]
    for at, copy in enumerate(copies):
        copy.start(priority=min(at, 1))
    total[...] = jnp.zeros(total.shape, total.dtype)
    for load in loads:
        load.wait()
    for k in range(depth):
        for s in range(slots):
            name = screen[k, s]
            aim[k * slots + s] = jnp.where(name >= 0, owner[0, jnp.maximum(name, 0)], targets)
    lhs = sides(raw[...])
    for k in range(depth):
        copies[k].wait()
        for s in range(slots):
            add_tile(lhs[k], tiles, aim, k * slots + s, total)
    lay_out(size, n_col, 0, [total], keep, send)


def add_tile(lhs, tiles, aim, i, total):
    t = aim[i]
    total[t] += jnp.dot(lhs, tiles[i], preferred_element_type=jnp.float32)


def late_kernel(size, count, *refs):
    others, (tiles, aim, out, keep, send, totals) = refs[:count], refs[count:]
    slots = aim.shape[0] // others[0].shape[1]
    totals[...] = jnp.zeros(totals.shape, totals.dtype)
    for h, raw in enumerate(others):
        lhs = sides(raw[...])
        for i in range(aim.shape[0]):
            add_tile(lhs[i // slots], tiles, aim, i, totals.at[h])
    lay_out(size, count + 1, 1, [totals.at[h] for h in range(count)], keep, send)
    encode([send[i] for i in range(4 * count)], out)


def early_sums_kernel(keep, got, ahead, out):
    sums = [keep[at] + got[at] for at in range(4)]
    encode(sums[1:3], ahead)
    out[0] = sums[0]
    out[1] = sums[3]


def near_kernel(n_col, early, late_keep, late_got, side, diagonal, out):
    rows, width = early.shape[1:]
    sums = []
    for at in range(4):
        sums.append([late_keep[i] + decode(late_got, i, rows, width) for i in range(at, (n_col - 1) * 4, 4)])
    encode(sums[1] + sums[2], side)
    encode([early[0]] + sums[0], diagonal)
    out[0] = early[1]
    for h in range(n_col - 1):
        out[1 + h] = sums[3][h]


def emit(groups, values, outs):
    at = 0
    for out, count in zip(outs, groups):
        if out is outs[-1]:
            for i in range(count):
                out[i] = values[at + i]
        else:
            encode(values[at : at + count], out)
        at += count


def pass_kernel(rows, each, ahead, side, out):
    late = (side.shape[0] // rows) // 2
    out[:rows, :] = ahead[rows : 2 * rows, :]
    out[rows : (1 + late) * rows, :] = side[late * rows : 2 * late * rows, :]
    first = ahead[ahead.shape[0] - SPARE :, :].astype(jnp.int32)[each : 2 * each]
    rest = side[2 * late * rows :, :].astype(jnp.int32)[late * each : 2 * late * each]
    last = out.shape[0] - (1 + late) * rows
    lines = [first, rest]
    if last > (1 + late) * each:
        lines.append(jnp.zeros((last - (1 + late) * each, LANES), jnp.int32))
    out[(1 + late) * rows :, :] = jnp.concatenate(lines, axis=0).astype(jnp.int16)


def sort_kernel(n_col, near, far, groups, keep, ahead, side, diagonal, passed, *refs):
    outs, sums = refs[:-1], refs[-1]
    rows, width = keep.shape[1:]
    for h in range(n_col):
        x = keep[h] + (decode(ahead, 0, rows, width) if h == 0 else decode(side, h - 1, rows, width))
        x = x + decode(passed, h, rows, width)
        sums[h] = x + decode(diagonal, h, rows, width)
    high, col = lax.axis_index("row") // near, lax.axis_index("col")
    emit(groups, [sums[lax.rem(col + n_col - (high ^ j), n_col)] for j in far], outs)


def far_kernel(groups, arrived, keep, *refs):
    coded, outs = refs[:arrived], refs[arrived:]
    rows, width = keep.shape[1:]
    values = []
    for i in range(sum(groups)):
        x = keep[i]
        for part in coded:
            x = x + decode(part, i, rows, width)
        values.append(x)
    emit(groups, values, outs)


def last_kernel(targets, size, keep, *refs):
    coded, out = refs[:-1], refs[-1]
    x = keep[0]
    for part in coded:
        x = x + decode(part, 0, targets * size, x.shape[1])
    for t in range(targets):
        out[:, t, :] = x[t * size : (t + 1) * size, :]


def offsets(masks):
    order = [0]
    for mask in masks:
        order = [mask | o for o in order] + order
    return order


def body(n_row, n_col, amplitudes, integrals, screen, owner_map):
    half, depth, width = amplitudes.shape
    slots, targets, out_width = integrals.shape[1], owner_map.shape[1], integrals.shape[3]
    size = half * n_col // n_row
    near = n_row // n_col
    spec = pl.BlockSpec(memory_space=pltpu.VMEM)
    smem = pl.BlockSpec(memory_space=pltpu.SMEM)
    hbm = pl.BlockSpec(memory_space=pltpu.HBM)
    params = pltpu.CompilerParams(vmem_limit_bytes=24 * 1024 * 1024)
    block = (targets * size, out_width)

    def vmem(x):
        return pltpu.with_memory_space_constraint(x, pltpu.VMEM)

    def swap(x, mask):
        return lax.ppermute(x, "row", [(i, i ^ mask) for i in range(n_row)])

    def call(kernel, name, out_shape, *operands, **more):
        single = not isinstance(out_shape, list)
        return pl.pallas_call(
            kernel,
            out_shape=out_shape,
            in_specs=[spec] * len(operands),
            out_specs=spec if single else [spec] * len(out_shape),
            compiler_params=params,
            name=name,
            **more,
        )(*[vmem(x) for x in operands])

    def coded(count, more=0):
        count *= out_width // LANES
        return pltpu.VMEM((count * block[0] + more + spare(count), LANES), jnp.int16)

    def kept(count):
        return pltpu.VMEM((count,) + block, jnp.float32)

    others = [
        lax.ppermute(amplitudes, "col", [(i, (i + step) % n_col) for i in range(n_col)])
        for step in range(1, n_col)
    ]
    half_cost = pl.CostEstimate(
        flops=2 * half * depth * targets * width * out_width, bytes_accessed=0, transcendentals=0
    )
    tiles, aim, send, keep = pl.pallas_call(
        functools.partial(early_kernel, size, n_col),
        out_shape=[
            pltpu.VMEM((depth * slots, width, out_width), jnp.bfloat16),
            pltpu.SMEM((depth * slots,), jnp.int32),
            kept(4),
            kept(4),
        ],
        in_specs=[hbm] * 4,
        out_specs=[spec, smem, spec, spec],
        scratch_shapes=[
            pltpu.SMEM(screen.shape, jnp.int32),
            pltpu.SMEM(owner_map.shape, jnp.int32),
            pltpu.VMEM(amplitudes.shape, jnp.bfloat16),
            pltpu.VMEM((targets + 1, half, out_width), jnp.float32),
            pltpu.SemaphoreType.DMA((depth,)),
            pltpu.SemaphoreType.DMA((3,)),
        ],
        cost_estimate=pl.CostEstimate(
            flops=half_cost.flops, bytes_accessed=integrals.size * 2, transcendentals=0
        ),
        compiler_params=params,
        name="early_half",
    )(*[pltpu.with_memory_space_constraint(x, pltpu.HBM) for x in (screen, owner_map, amplitudes, integrals)])
    got = swap(send, 1)

    lates = n_col - 1
    late_send, late_keep = pl.pallas_call(
        functools.partial(late_kernel, size, lates),
        out_shape=[coded(lates * 4), kept(lates * 4)],
        in_specs=[spec] * n_col + [smem],
        out_specs=[spec, spec],
        scratch_shapes=[
            pltpu.VMEM((lates * 4,) + block, jnp.float32),
            pltpu.VMEM((lates, targets + 1, half, out_width), jnp.float32),
        ],
        cost_estimate=half_cost,
        compiler_params=params,
        name="late_half",
    )(*[vmem(o) for o in others], vmem(tiles), pltpu.with_memory_space_constraint(aim, pltpu.SMEM))
    late_got = swap(late_send, 1)
    def to_side(x):
        return lax.ppermute(x, "row", [(i, i ^ (ALONG if i % 2 else ACROSS) ^ 1) for i in range(n_row)])

    ahead, early = call(early_sums_kernel, "early_sums", [coded(2, SPARE), kept(2)], keep, got)
    ahead = to_side(ahead)
    side, diagonal, keep = call(
        functools.partial(near_kernel, n_col),
        "near_sums",
        [coded(2 * lates), coded(n_col), kept(n_col)],
        early,
        late_keep,
        late_got,
    )
    side = to_side(side)
    diagonal = swap(diagonal, ACROSS | ALONG | 1)
    each = out_width // LANES
    passed = call(functools.partial(pass_kernel, each * block[0], each), "pass_on", coded(n_col), ahead, side)
    arrived = [ahead, side, diagonal, swap(passed, 1)]

    masks = [near << b for b in range(n_col.bit_length() - 1)]
    plans, far = [], [0]
    for stage in reversed(pairs_of(masks)):
        partners = offsets(stage)
        plans.insert(0, (partners, len(far)))
        far = [p | o for p in partners for o in far]
    for at, (partners, count) in enumerate(plans):
        groups = [count] * len(partners)
        if at == 0:
            offs = [o // near for o in far]
            kernel = functools.partial(sort_kernel, n_col, near, offs, groups)
            more = dict(scratch_shapes=[pltpu.VMEM((n_col,) + block, jnp.float32)])
        else:
            kernel, more = functools.partial(far_kernel, groups, len(arrived)), {}
        *parts, keep = call(
            kernel, "far_sums", [coded(count)] * (len(partners) - 1) + [kept(count)], keep, *arrived, **more
        )
        arrived = [swap(part, partner | 1) for part, partner in zip(parts, partners)]
    return pl.pallas_call(
        functools.partial(last_kernel, targets, size),
        out_shape=jax.ShapeDtypeStruct((size, targets, out_width), jnp.float32),
        in_specs=[spec] * (1 + len(arrived)),
        out_specs=spec,
        compiler_params=params,
        name="own_block",
    )(vmem(keep), *[vmem(part) for part in arrived])


def solution(mesh):
    return jax.shard_map(
        functools.partial(body, mesh.shape["row"], mesh.shape["col"]),
        mesh=mesh,
        in_specs=(
            P("col", "row", None),
            P("row", "col", None, None),
            P("row", "col"),
            P("col", None),
        ),
        out_specs=P("row", "col", None),
        check_vma=False,
    )
```

```python
import functools

import jax
import jax.numpy as jnp
from jax import lax
from jax.experimental import pallas as pl
from jax.experimental.pallas import tpu as pltpu
from jax.sharding import PartitionSpec as P

SPARE = 16
LEAST = -100
LANES = 128
ACROSS, ALONG = 2, 4


def place(size, total, places):
    targets, near = total.shape[0] - 1, total.shape[1] // size
    low = lax.rem(lax.axis_index("row"), near)
    for ref, at, offset in places:
        first = pl.multiple_of((low ^ offset) * size, size)
        for t in range(targets):
            ref[at, t * size : (t + 1) * size, :] = total[t, pl.ds(first, size), :]


def pairs_of(masks):
    return [masks[at : at + 2] for at in range(0, len(masks), 2)]


def lay_out(size, n_col, step, totals, keep, send):
    row, col = lax.axis_index("row"), lax.axis_index("col")
    second = lax.rem(row, 2) == 1
    mine, other = jnp.where(second, ALONG, ACROSS), jnp.where(second, ACROSS, ALONG)
    near = totals[0].shape[1] // size
    for h, total in enumerate(totals):
        offset = (row // near) ^ lax.rem(col + n_col - step - h, n_col)
        flip = 0
        for stage in pairs_of([1 << b for b in range(n_col.bit_length() - 1)]):
            flip = flip ^ jnp.where(offset & sum(stage) != 0, 1, 0)
        kept = (ACROSS | ALONG | 1, mine ^ 1, mine, 0)
        sent = (ACROSS | ALONG, other, other ^ 1, 1)
        places = [(keep, 4 * h + at, j ^ flip) for at, j in enumerate(kept)]
        place(size, total, places + [(send, 4 * h + at, j ^ flip) for at, j in enumerate(sent)])


def sides(raw):
    by_tile = jnp.swapaxes(raw, 0, 1)
    return [by_tile[k] for k in range(by_tile.shape[0])]


def spare(count):
    return -(-count // SPARE) * SPARE


def encode(values, out):
    rows, width = values[0].shape
    pieces = [x[:, c : c + LANES] for x in values for c in range(0, width, LANES)]
    last = spare(len(pieces))
    at_row = lax.broadcasted_iota(jnp.int32, (last, LANES), 0)
    exponents = jnp.zeros((last, LANES), jnp.int32)
    for at, x in enumerate(pieces):
        largest = jnp.maximum(jnp.max(jnp.abs(x), axis=0, keepdims=True), 2.0**LEAST)
        exponent = jnp.floor(jnp.log2(largest)) + 1.0
        code = jnp.round(x * jnp.exp2(15.0 - exponent))
        code = jnp.clip(code, -32767.0, 32767.0).astype(jnp.int32)
        out[at * rows : (at + 1) * rows, :] = code.astype(jnp.int16)
        exponents = jnp.where(at_row == at, exponent.astype(jnp.int32), exponents)
    data = len(pieces) * rows
    for at in range(data, out.shape[0] - last, SPARE):
        out[at : at + SPARE, :] = jnp.zeros((SPARE, LANES), jnp.int16)
    out[out.shape[0] - last :, :] = exponents.astype(jnp.int16)


def decode(coded, at, rows, width):
    each = width // LANES
    count = coded.shape[0] // rows
    exponents = coded[coded.shape[0] - spare(count) :, :].astype(jnp.int32)
    parts = []
    for i in range(at * each, (at + 1) * each):
        code = coded[i * rows : (i + 1) * rows, :].astype(jnp.int32).astype(jnp.float32)
        parts.append(code * jnp.exp2(exponents[i : i + 1, :].astype(jnp.float32) - 15.0))
    return jnp.concatenate(parts, axis=1)


def early_kernel(
    size, n_col, screen_hbm, owner_hbm, own_hbm, integrals,
    tiles, aim, send, keep, screen, owner, raw, total, sems, small,
):
    depth, slots = screen.shape
    targets = owner.shape[1]
    loads = [
        pltpu.make_async_copy(src, dst, small.at[at])
        for at, (src, dst) in enumerate(((screen_hbm, screen), (owner_hbm, owner), (own_hbm, raw)))
    ]

    for load in loads:
        load.start()
    copies = [
        pltpu.make_async_copy(integrals.at[k], tiles.at[pl.ds(k * slots, slots)], sems.at[k]) for k in range(depth)
    ]
    for at, copy in enumerate(copies):
        copy.start(priority=min(at, 1))
    total[...] = jnp.zeros(total.shape, total.dtype)
    for load in loads:
        load.wait()
    for k in range(depth):
        for s in range(slots):
            name = screen[k, s]
            aim[k * slots + s] = jnp.where(name >= 0, owner[0, jnp.maximum(name, 0)], targets)
    lhs = sides(raw[...])
    for k in range(depth):
        copies[k].wait()
        for s in range(slots):
            add_tile(lhs[k], tiles, aim, k * slots + s, total)
    lay_out(size, n_col, 0, [total], keep, send)


def add_tile(lhs, tiles, aim, i, total):
    t = aim[i]
    total[t] += jnp.dot(lhs, tiles[i], preferred_element_type=jnp.float32)


def late_kernel(size, count, *refs):
    others, (tiles, aim, send, keep, totals) = refs[:count], refs[count:]
    slots = aim.shape[0] // others[0].shape[1]
    totals[...] = jnp.zeros(totals.shape, totals.dtype)
    for h, raw in enumerate(others):
        lhs = sides(raw[...])
        for i in range(aim.shape[0]):
            add_tile(lhs[i // slots], tiles, aim, i, totals.at[h])
    lay_out(size, count + 1, 1, [totals.at[h] for h in range(count)], keep, send)


def early_sums_kernel(keep, got, ahead, out):
    sums = [keep[at] + got[at] for at in range(4)]
    encode(sums[1:3], ahead)
    out[0] = sums[0]
    out[1] = sums[3]


def near_kernel(n_col, early, late_keep, late_got, side, diagonal, out):
    rows, width = early.shape[1:]
    sums = []
    for at in range(4):
        sums.append([late_keep[i] + late_got[i] for i in range(at, (n_col - 1) * 4, 4)])
    encode(sums[1] + sums[2], side)
    encode([early[0]] + sums[0], diagonal)
    out[0] = early[1]
    for h in range(n_col - 1):
        out[1 + h] = sums[3][h]


def emit(groups, values, outs):
    at = 0
    for out, count in zip(outs, groups):
        if out is outs[-1]:
            for i in range(count):
                out[i] = values[at + i]
        else:
            encode(values[at : at + count], out)
        at += count


def pass_kernel(rows, each, ahead, side, out):
    late = (side.shape[0] // rows) // 2
    out[:rows, :] = ahead[rows : 2 * rows, :]
    out[rows : (1 + late) * rows, :] = side[late * rows : 2 * late * rows, :]
    first = ahead[ahead.shape[0] - SPARE :, :].astype(jnp.int32)[each : 2 * each]
    rest = side[2 * late * rows :, :].astype(jnp.int32)[late * each : 2 * late * each]
    last = out.shape[0] - (1 + late) * rows
    lines = [first, rest]
    if last > (1 + late) * each:
        lines.append(jnp.zeros((last - (1 + late) * each, LANES), jnp.int32))
    out[(1 + late) * rows :, :] = jnp.concatenate(lines, axis=0).astype(jnp.int16)


def sort_kernel(n_col, near, far, groups, keep, ahead, side, diagonal, passed, *refs):
    outs, sums = refs[:-1], refs[-1]
    rows, width = keep.shape[1:]
    for h in range(n_col):
        x = keep[h] + (decode(ahead, 0, rows, width) if h == 0 else decode(side, h - 1, rows, width))
        x = x + decode(passed, h, rows, width)
        sums[h] = x + decode(diagonal, h, rows, width)
    high, col = lax.axis_index("row") // near, lax.axis_index("col")
    emit(groups, [sums[lax.rem(col + n_col - (high ^ j), n_col)] for j in far], outs)


def far_kernel(groups, arrived, keep, *refs):
    coded, outs = refs[:arrived], refs[arrived:]
    rows, width = keep.shape[1:]
    values = []
    for i in range(sum(groups)):
        x = keep[i]
        for part in coded:
            x = x + decode(part, i, rows, width)
        values.append(x)
    emit(groups, values, outs)


def last_kernel(targets, size, keep, *refs):
    coded, out = refs[:-1], refs[-1]
    x = keep[0]
    for part in coded:
        x = x + decode(part, 0, targets * size, x.shape[1])
    for t in range(targets):
        out[:, t, :] = x[t * size : (t + 1) * size, :]


def offsets(masks):
    order = [0]
    for mask in masks:
        order = [mask | o for o in order] + order
    return order


def body(n_row, n_col, amplitudes, integrals, screen, owner_map):
    half, depth, width = amplitudes.shape
    slots, targets, out_width = integrals.shape[1], owner_map.shape[1], integrals.shape[3]
    size = half * n_col // n_row
    near = n_row // n_col
    spec = pl.BlockSpec(memory_space=pltpu.VMEM)
    smem = pl.BlockSpec(memory_space=pltpu.SMEM)
    hbm = pl.BlockSpec(memory_space=pltpu.HBM)
    params = pltpu.CompilerParams(vmem_limit_bytes=24 * 1024 * 1024)
    block = (targets * size, out_width)

    def vmem(x):
        return pltpu.with_memory_space_constraint(x, pltpu.VMEM)

    def swap(x, mask):
        return lax.ppermute(x, "row", [(i, i ^ mask) for i in range(n_row)])

    def call(kernel, name, out_shape, *operands, **more):
        single = not isinstance(out_shape, list)
        return pl.pallas_call(
            kernel,
            out_shape=out_shape,
            in_specs=[spec] * len(operands),
            out_specs=spec if single else [spec] * len(out_shape),
            compiler_params=params,
            name=name,
            **more,
        )(*[vmem(x) for x in operands])

    def coded(count, more=0):
        count *= out_width // LANES
        return pltpu.VMEM((count * block[0] + more + spare(count), LANES), jnp.int16)

    def kept(count):
        return pltpu.VMEM((count,) + block, jnp.float32)

    others = [
        lax.ppermute(amplitudes, "col", [(i, (i + step) % n_col) for i in range(n_col)])
        for step in range(1, n_col)
    ]
    half_cost = pl.CostEstimate(
        flops=2 * half * depth * targets * width * out_width, bytes_accessed=0, transcendentals=0
    )
    tiles, aim, send, keep = pl.pallas_call(
        functools.partial(early_kernel, size, n_col),
        out_shape=[
            pltpu.VMEM((depth * slots, width, out_width), jnp.bfloat16),
            pltpu.SMEM((depth * slots,), jnp.int32),
            kept(4),
            kept(4),
        ],
        in_specs=[hbm] * 4,
        out_specs=[spec, smem, spec, spec],
        scratch_shapes=[
            pltpu.SMEM(screen.shape, jnp.int32),
            pltpu.SMEM(owner_map.shape, jnp.int32),
            pltpu.VMEM(amplitudes.shape, jnp.bfloat16),
            pltpu.VMEM((targets + 1, half, out_width), jnp.float32),
            pltpu.SemaphoreType.DMA((depth,)),
            pltpu.SemaphoreType.DMA((3,)),
        ],
        cost_estimate=pl.CostEstimate(
            flops=half_cost.flops, bytes_accessed=integrals.size * 2, transcendentals=0
        ),
        compiler_params=params,
        name="early_half",
    )(*[pltpu.with_memory_space_constraint(x, pltpu.HBM) for x in (screen, owner_map, amplitudes, integrals)])
    got = swap(send, 1)

    lates = n_col - 1
    late_send, late_keep = pl.pallas_call(
        functools.partial(late_kernel, size, lates),
        out_shape=[kept(lates * 4), kept(lates * 4)],
        in_specs=[spec] * n_col + [smem],
        out_specs=[spec, spec],
        scratch_shapes=[
            pltpu.VMEM((lates, targets + 1, half, out_width), jnp.float32),
        ],
        cost_estimate=half_cost,
        compiler_params=params,
        name="late_half",
    )(*[vmem(o) for o in others], vmem(tiles), pltpu.with_memory_space_constraint(aim, pltpu.SMEM))
    late_got = swap(late_send, 1)
    def to_side(x):
        return lax.ppermute(x, "row", [(i, i ^ (ALONG if i % 2 else ACROSS) ^ 1) for i in range(n_row)])

    ahead, early = call(early_sums_kernel, "early_sums", [coded(2, SPARE), kept(2)], keep, got)
    ahead = to_side(ahead)
    side, diagonal, keep = call(
        functools.partial(near_kernel, n_col),
        "near_sums",
        [coded(2 * lates), coded(n_col), kept(n_col)],
        early,
        late_keep,
        late_got,
    )
    side = to_side(side)
    diagonal = swap(diagonal, ACROSS | ALONG | 1)
    each = out_width // LANES
    passed = call(functools.partial(pass_kernel, each * block[0], each), "pass_on", coded(n_col), ahead, side)
    arrived = [ahead, side, diagonal, swap(passed, 1)]

    masks = [near << b for b in range(n_col.bit_length() - 1)]
    plans, far = [], [0]
    for stage in reversed(pairs_of(masks)):
        partners = offsets(stage)
        plans.insert(0, (partners, len(far)))
        far = [p | o for p in partners for o in far]
    for at, (partners, count) in enumerate(plans):
        groups = [count] * len(partners)
        if at == 0:
            offs = [o // near for o in far]
            kernel = functools.partial(sort_kernel, n_col, near, offs, groups)
            more = dict(scratch_shapes=[pltpu.VMEM((n_col,) + block, jnp.float32)])
        else:
            kernel, more = functools.partial(far_kernel, groups, len(arrived)), {}
        *parts, keep = call(
            kernel, "far_sums", [coded(count)] * (len(partners) - 1) + [kept(count)], keep, *arrived, **more
        )
        arrived = [swap(part, partner | 1) for part, partner in zip(parts, partners)]
    return pl.pallas_call(
        functools.partial(last_kernel, targets, size),
        out_shape=jax.ShapeDtypeStruct((size, targets, out_width), jnp.float32),
        in_specs=[spec] * (1 + len(arrived)),
        out_specs=spec,
        compiler_params=params,
        name="own_block",
    )(vmem(keep), *[vmem(part) for part in arrived])


def solution(mesh):
    return jax.shard_map(
        functools.partial(body, mesh.shape["row"], mesh.shape["col"]),
        mesh=mesh,
        in_specs=(
            P("col", "row", None),
            P("row", "col", None, None),
            P("row", "col"),
            P("col", None),
        ),
        out_specs=P("row", "col", None),
        check_vma=False,
    )
```

```python
import functools

import jax
import jax.numpy as jnp
from jax import lax
from jax.experimental import pallas as pl
from jax.experimental.pallas import tpu as pltpu
from jax.sharding import PartitionSpec as P

SPARE = 16
LEAST = -100
LANES = 128
PARTS = (3, 4, 5, 6)
ACROSS, ALONG = 2, 4


def place(size, total, places):
    targets, near = total.shape[0] - 1, total.shape[1] // size
    low = lax.rem(lax.axis_index("row"), near)
    for ref, at, offset in places:
        first = pl.multiple_of((low ^ offset) * size, size)
        for t in range(targets):
            ref[at, t * size : (t + 1) * size, :] = total[t, pl.ds(first, size), :]


def pairs_of(masks):
    return [masks[at : at + 2] for at in range(0, len(masks), 2)]


def lay_out(size, n_col, step, totals, keep, send):
    row, col = lax.axis_index("row"), lax.axis_index("col")
    second = lax.rem(row, 2) == 1
    mine, other = jnp.where(second, ALONG, ACROSS), jnp.where(second, ACROSS, ALONG)
    near = totals[0].shape[1] // size
    for h, total in enumerate(totals):
        offset = (row // near) ^ lax.rem(col + n_col - step - h, n_col)
        flip = 0
        for stage in pairs_of([1 << b for b in range(n_col.bit_length() - 1)]):
            flip = flip ^ jnp.where(offset & sum(stage) != 0, 1, 0)
        kept = (ACROSS | ALONG | 1, mine ^ 1, mine, 0)
        sent = (ACROSS | ALONG, other, other ^ 1, 1)
        places = [(keep, 4 * h + at, j ^ flip) for at, j in enumerate(kept)]
        place(size, total, places + [(send, 4 * h + at, j ^ flip) for at, j in enumerate(sent)])


def sides(raw):
    by_tile = jnp.swapaxes(raw, 0, 1)
    return [by_tile[k] for k in range(by_tile.shape[0])]


def spare(count):
    return -(-count // SPARE) * SPARE


def encode(values, out):
    rows, width = values[0].shape
    pieces = [x[:, c : c + LANES] for x in values for c in range(0, width, LANES)]
    last = spare(len(pieces))
    at_row = lax.broadcasted_iota(jnp.int32, (last, LANES), 0)
    exponents = jnp.zeros((last, LANES), jnp.int32)
    for at, x in enumerate(pieces):
        largest = jnp.maximum(jnp.max(jnp.abs(x), axis=0, keepdims=True), 2.0**LEAST)
        exponent = jnp.floor(jnp.log2(largest)) + 1.0
        code = jnp.round(x * jnp.exp2(15.0 - exponent))
        code = jnp.clip(code, -32767.0, 32767.0).astype(jnp.int32)
        out[at * rows : (at + 1) * rows, :] = code.astype(jnp.int16)
        exponents = jnp.where(at_row == at, exponent.astype(jnp.int32), exponents)
    data = len(pieces) * rows
    for at in range(data, out.shape[0] - last, SPARE):
        out[at : at + SPARE, :] = jnp.zeros((SPARE, LANES), jnp.int16)
    out[out.shape[0] - last :, :] = exponents.astype(jnp.int16)


def decode(coded, at, rows, width):
    each = width // LANES
    count = coded.shape[0] // rows
    exponents = coded[coded.shape[0] - spare(count) :, :].astype(jnp.int32)
    parts = []
    for i in range(at * each, (at + 1) * each):
        code = coded[i * rows : (i + 1) * rows, :].astype(jnp.int32).astype(jnp.float32)
        parts.append(code * jnp.exp2(exponents[i : i + 1, :].astype(jnp.float32) - 15.0))
    return jnp.concatenate(parts, axis=1)


def list_live(screen, owner, live):
    depth, slots = screen.shape
    end = depth * slots
    for at in range(end):
        for n, value in enumerate((0, 0, owner.shape[1])):
            live[n * (end + 1) + at] = value
    count = 0
    for k in range(depth):
        for s in range(slots):
            name = screen[k, s]
            at = jnp.where(name >= 0, count, end)
            for n, value in enumerate((k * slots + s, k, owner[0, jnp.maximum(name, 0)])):
                live[n * (end + 1) + at] = value
            count = count + jnp.where(name >= 0, 1, 0)
    live[end] = count


def early_kernel(
    size, n_col, screen_hbm, owner_hbm, own_hbm, integrals,
    tiles, live, send, keep, screen, owner, aim, raw, total, sems, small,
):
    depth, slots = screen.shape
    targets = owner.shape[1]
    loads = [
        pltpu.make_async_copy(src, dst, small.at[at])
        for at, (src, dst) in enumerate(((screen_hbm, screen), (owner_hbm, owner), (own_hbm, raw)))
    ]

    for load in loads:
        load.start()
    copies = [
        pltpu.make_async_copy(integrals.at[k], tiles.at[pl.ds(k * slots, slots)], sems.at[k]) for k in range(depth)
    ]
    for at, copy in enumerate(copies):
        copy.start(priority=min(at, 1))
    total[...] = jnp.zeros(total.shape, total.dtype)
    for load in loads:
        load.wait()
    for k in range(depth):
        for s in range(slots):
            name = screen[k, s]
            aim[k * slots + s] = jnp.where(name >= 0, owner[0, jnp.maximum(name, 0)], targets)
    list_live(screen, owner, live)
    lhs = sides(raw[...])
    for k in range(depth):
        copies[k].wait()
        for s in range(slots):
            add_tile(lhs[k], tiles, aim, k * slots + s, total)
    lay_out(size, n_col, 0, [total], keep, send)


def add_tile(lhs, tiles, aim, i, total):
    t = aim[i]
    total[t] += jnp.dot(lhs, tiles[i], preferred_element_type=jnp.float32)


def late_kernel(size, count, *refs):
    others, (tiles, live, send, keep, lhs, totals) = refs[:count], refs[count:]
    slots = tiles.shape[0]
    totals[...] = jnp.zeros(totals.shape, totals.dtype)
    for h, raw in enumerate(others):
        for k, side in enumerate(sides(raw[...])):
            lhs[k, h] = side
    sizes = [0] + [slots * part // 6 for part in PARTS]
    for low, high in zip(sizes, sizes[1:]):

        @pl.when(jnp.logical_and(live[slots] > low, live[slots] <= high))
        def _():
            for h in range(count):
                for i in range(high):
                    tile, k, t = (live[n * (slots + 1) + i] for n in range(3))
                    totals[h, t] += jnp.dot(lhs[k, h], tiles[tile], preferred_element_type=jnp.float32)

    lay_out(size, count + 1, 1, [totals.at[h] for h in range(count)], keep, send)


def early_sums_kernel(keep, got, ahead, out):
    sums = [keep[at] + got[at] for at in range(4)]
    encode(sums[1:3], ahead)
    out[0] = sums[0]
    out[1] = sums[3]


def near_kernel(n_col, early, late_keep, late_got, side, diagonal, out):
    rows, width = early.shape[1:]
    sums = []
    for at in range(4):
        sums.append([late_keep[i] + late_got[i] for i in range(at, (n_col - 1) * 4, 4)])
    encode(sums[1] + sums[2], side)
    encode([early[0]] + sums[0], diagonal)
    out[0] = early[1]
    for h in range(n_col - 1):
        out[1 + h] = sums[3][h]


def emit(groups, values, outs):
    at = 0
    for out, count in zip(outs, groups):
        if out is outs[-1]:
            for i in range(count):
                out[i] = values[at + i]
        else:
            encode(values[at : at + count], out)
        at += count


def pass_kernel(rows, each, ahead, side, out):
    late = (side.shape[0] // rows) // 2
    out[:rows, :] = ahead[rows : 2 * rows, :]
    out[rows : (1 + late) * rows, :] = side[late * rows : 2 * late * rows, :]
    first = ahead[ahead.shape[0] - SPARE :, :].astype(jnp.int32)[each : 2 * each]
    rest = side[2 * late * rows :, :].astype(jnp.int32)[late * each : 2 * late * each]
    last = out.shape[0] - (1 + late) * rows
    lines = [first, rest]
    if last > (1 + late) * each:
        lines.append(jnp.zeros((last - (1 + late) * each, LANES), jnp.int32))
    out[(1 + late) * rows :, :] = jnp.concatenate(lines, axis=0).astype(jnp.int16)


def sort_kernel(n_col, near, far, groups, keep, ahead, side, diagonal, passed, *refs):
    outs, sums = refs[:-1], refs[-1]
    rows, width = keep.shape[1:]
    for h in range(n_col):
        x = keep[h] + (decode(ahead, 0, rows, width) if h == 0 else decode(side, h - 1, rows, width))
        x = x + decode(passed, h, rows, width)
        sums[h] = x + decode(diagonal, h, rows, width)
    high, col = lax.axis_index("row") // near, lax.axis_index("col")
    emit(groups, [sums[lax.rem(col + n_col - (high ^ j), n_col)] for j in far], outs)


def far_kernel(groups, arrived, keep, *refs):
    coded, outs = refs[:arrived], refs[arrived:]
    rows, width = keep.shape[1:]
    values = []
    for i in range(sum(groups)):
        x = keep[i]
        for part in coded:
            x = x + decode(part, i, rows, width)
        values.append(x)
    emit(groups, values, outs)


def last_kernel(targets, size, keep, *refs):
    coded, out = refs[:-1], refs[-1]
    x = keep[0]
    for part in coded:
        x = x + decode(part, 0, targets * size, x.shape[1])
    for t in range(targets):
        out[:, t, :] = x[t * size : (t + 1) * size, :]


def offsets(masks):
    order = [0]
    for mask in masks:
        order = [mask | o for o in order] + order
    return order


def body(n_row, n_col, amplitudes, integrals, screen, owner_map):
    half, depth, width = amplitudes.shape
    slots, targets, out_width = integrals.shape[1], owner_map.shape[1], integrals.shape[3]
    size = half * n_col // n_row
    near = n_row // n_col
    spec = pl.BlockSpec(memory_space=pltpu.VMEM)
    smem = pl.BlockSpec(memory_space=pltpu.SMEM)
    hbm = pl.BlockSpec(memory_space=pltpu.HBM)
    params = pltpu.CompilerParams(vmem_limit_bytes=24 * 1024 * 1024)
    block = (targets * size, out_width)

    def vmem(x):
        return pltpu.with_memory_space_constraint(x, pltpu.VMEM)

    def swap(x, mask):
        return lax.ppermute(x, "row", [(i, i ^ mask) for i in range(n_row)])

    def call(kernel, name, out_shape, *operands, **more):
        single = not isinstance(out_shape, list)
        return pl.pallas_call(
            kernel,
            out_shape=out_shape,
            in_specs=[spec] * len(operands),
            out_specs=spec if single else [spec] * len(out_shape),
            compiler_params=params,
            name=name,
            **more,
        )(*[vmem(x) for x in operands])

    def coded(count, more=0):
        count *= out_width // LANES
        return pltpu.VMEM((count * block[0] + more + spare(count), LANES), jnp.int16)

    def kept(count):
        return pltpu.VMEM((count,) + block, jnp.float32)

    others = [
        lax.ppermute(amplitudes, "col", [(i, (i + step) % n_col) for i in range(n_col)])
        for step in range(1, n_col)
    ]
    half_cost = pl.CostEstimate(
        flops=2 * half * depth * targets * width * out_width, bytes_accessed=0, transcendentals=0
    )
    tiles, live, send, keep = pl.pallas_call(
        functools.partial(early_kernel, size, n_col),
        out_shape=[
            pltpu.VMEM((depth * slots, width, out_width), jnp.bfloat16),
            pltpu.SMEM((3 * (depth * slots + 1),), jnp.int32),
            kept(4),
            kept(4),
        ],
        in_specs=[hbm] * 4,
        out_specs=[spec, smem, spec, spec],
        scratch_shapes=[
            pltpu.SMEM(screen.shape, jnp.int32),
            pltpu.SMEM(owner_map.shape, jnp.int32),
            pltpu.SMEM((depth * slots,), jnp.int32),
            pltpu.VMEM(amplitudes.shape, jnp.bfloat16),
            pltpu.VMEM((targets + 1, half, out_width), jnp.float32),
            pltpu.SemaphoreType.DMA((depth,)),
            pltpu.SemaphoreType.DMA((3,)),
        ],
        cost_estimate=pl.CostEstimate(
            flops=half_cost.flops, bytes_accessed=integrals.size * 2, transcendentals=0
        ),
        compiler_params=params,
        name="early_half",
    )(*[pltpu.with_memory_space_constraint(x, pltpu.HBM) for x in (screen, owner_map, amplitudes, integrals)])
    got = swap(send, 1)

    lates = n_col - 1
    late_send, late_keep = pl.pallas_call(
        functools.partial(late_kernel, size, lates),
        out_shape=[kept(lates * 4), kept(lates * 4)],
        in_specs=[spec] * n_col + [smem],
        out_specs=[spec, spec],
        scratch_shapes=[
            pltpu.VMEM((depth, lates, half, width), jnp.bfloat16),
            pltpu.VMEM((lates, targets + 1, half, out_width), jnp.float32),
        ],
        cost_estimate=half_cost,
        compiler_params=params,
        name="late_half",
    )(*[vmem(o) for o in others], vmem(tiles), pltpu.with_memory_space_constraint(live, pltpu.SMEM))
    late_got = swap(late_send, 1)
    def to_side(x):
        return lax.ppermute(x, "row", [(i, i ^ (ALONG if i % 2 else ACROSS) ^ 1) for i in range(n_row)])

    ahead, early = call(early_sums_kernel, "early_sums", [coded(2, SPARE), kept(2)], keep, got)
    ahead = to_side(ahead)
    side, diagonal, keep = call(
        functools.partial(near_kernel, n_col),
        "near_sums",
        [coded(2 * lates), coded(n_col), kept(n_col)],
        early,
        late_keep,
        late_got,
    )
    side = to_side(side)
    diagonal = swap(diagonal, ACROSS | ALONG | 1)
    each = out_width // LANES
    passed = call(functools.partial(pass_kernel, each * block[0], each), "pass_on", coded(n_col), ahead, side)
    arrived = [ahead, side, diagonal, swap(passed, 1)]

    masks = [near << b for b in range(n_col.bit_length() - 1)]
    plans, far = [], [0]
    for stage in reversed(pairs_of(masks)):
        partners = offsets(stage)
        plans.insert(0, (partners, len(far)))
        far = [p | o for p in partners for o in far]
    for at, (partners, count) in enumerate(plans):
        groups = [count] * len(partners)
        if at == 0:
            offs = [o // near for o in far]
            kernel = functools.partial(sort_kernel, n_col, near, offs, groups)
            more = dict(scratch_shapes=[pltpu.VMEM((n_col,) + block, jnp.float32)])
        else:
            kernel, more = functools.partial(far_kernel, groups, len(arrived)), {}
        *parts, keep = call(
            kernel, "far_sums", [coded(count)] * (len(partners) - 1) + [kept(count)], keep, *arrived, **more
        )
        arrived = [swap(part, partner | 1) for part, partner in zip(parts, partners)]
    return pl.pallas_call(
        functools.partial(last_kernel, targets, size),
        out_shape=jax.ShapeDtypeStruct((size, targets, out_width), jnp.float32),
        in_specs=[spec] * (1 + len(arrived)),
        out_specs=spec,
        compiler_params=params,
        name="own_block",
    )(vmem(keep), *[vmem(part) for part in arrived])


def solution(mesh):
    return jax.shard_map(
        functools.partial(body, mesh.shape["row"], mesh.shape["col"]),
        mesh=mesh,
        in_specs=(
            P("col", "row", None),
            P("row", "col", None, None),
            P("row", "col"),
            P("col", None),
        ),
        out_specs=P("row", "col", None),
        check_vma=False,
    )
```

```python
import functools

import jax
import jax.numpy as jnp
from jax import lax
from jax.experimental import pallas as pl
from jax.experimental.pallas import tpu as pltpu
from jax.sharding import PartitionSpec as P

SPARE = 16
LEAST = -100
LANES = 128
ACROSS, ALONG = 2, 4


def place(size, total, places):
    targets, near = total.shape[0] - 1, total.shape[1] // size
    low = lax.rem(lax.axis_index("row"), near)
    for ref, at, offset in places:
        first = pl.multiple_of((low ^ offset) * size, size)
        for t in range(targets):
            ref[at, t * size : (t + 1) * size, :] = total[t, pl.ds(first, size), :]


def pairs_of(masks):
    return [masks[at : at + 2] for at in range(0, len(masks), 2)]


def lay_out(size, n_col, step, totals, keep, send):
    row, col = lax.axis_index("row"), lax.axis_index("col")
    second = lax.rem(row, 2) == 1
    mine, other = jnp.where(second, ALONG, ACROSS), jnp.where(second, ACROSS, ALONG)
    near = totals[0].shape[1] // size
    for h, total in enumerate(totals):
        offset = (row // near) ^ lax.rem(col + n_col - step - h, n_col)
        flip = 0
        for stage in pairs_of([1 << b for b in range(n_col.bit_length() - 1)]):
            flip = flip ^ jnp.where(offset & sum(stage) != 0, 1, 0)
        kept = (ACROSS | ALONG | 1, mine ^ 1, mine, 0)
        sent = (ACROSS | ALONG, other, other ^ 1, 1)
        places = [(keep, 4 * h + at, j ^ flip) for at, j in enumerate(kept)]
        place(size, total, places + [(send, 4 * h + at, j ^ flip) for at, j in enumerate(sent)])


def sides(raw):
    by_tile = jnp.swapaxes(raw, 0, 1)
    return [by_tile[k] for k in range(by_tile.shape[0])]


def spare(count):
    return -(-count // SPARE) * SPARE


def encode(values, out):
    rows, width = values[0].shape
    pieces = [x[:, c : c + LANES] for x in values for c in range(0, width, LANES)]
    last = spare(len(pieces))
    at_row = lax.broadcasted_iota(jnp.int32, (last, LANES), 0)
    exponents = jnp.zeros((last, LANES), jnp.int32)
    for at, x in enumerate(pieces):
        largest = jnp.maximum(jnp.max(jnp.abs(x), axis=0, keepdims=True), 2.0**LEAST)
        exponent = jnp.floor(jnp.log2(largest)) + 1.0
        code = jnp.round(x * jnp.exp2(15.0 - exponent))
        code = jnp.clip(code, -32767.0, 32767.0).astype(jnp.int32)
        out[at * rows : (at + 1) * rows, :] = code.astype(jnp.int16)
        exponents = jnp.where(at_row == at, exponent.astype(jnp.int32), exponents)
    data = len(pieces) * rows
    for at in range(data, out.shape[0] - last, SPARE):
        out[at : at + SPARE, :] = jnp.zeros((SPARE, LANES), jnp.int16)
    out[out.shape[0] - last :, :] = exponents.astype(jnp.int16)


def decode(coded, at, rows, width):
    each = width // LANES
    count = coded.shape[0] // rows
    exponents = coded[coded.shape[0] - spare(count) :, :].astype(jnp.int32)
    parts = []
    for i in range(at * each, (at + 1) * each):
        code = coded[i * rows : (i + 1) * rows, :].astype(jnp.int32).astype(jnp.float32)
        parts.append(code * jnp.exp2(exponents[i : i + 1, :].astype(jnp.float32) - 15.0))
    return jnp.concatenate(parts, axis=1)


def early_kernel(
    size, n_col, screen_hbm, owner_hbm, own_hbm, integrals,
    tiles, aim, send, keep, screen, owner, raw, total, sems, small,
):
    depth, slots = screen.shape
    targets = owner.shape[1]
    loads = [
        pltpu.make_async_copy(src, dst, small.at[at])
        for at, (src, dst) in enumerate(((screen_hbm, screen), (owner_hbm, owner), (own_hbm, raw)))
    ]

    for load in loads:
        load.start()
    copies = [
        pltpu.make_async_copy(integrals.at[k], tiles.at[pl.ds(k * slots, slots)], sems.at[k]) for k in range(depth)
    ]
    for at, copy in enumerate(copies):
        copy.start(priority=min(at, 1))
    total[...] = jnp.zeros(total.shape, total.dtype)
    for load in loads:
        load.wait()
    for k in range(depth):
        for s in range(slots):
            name = screen[k, s]
            aim[k * slots + s] = jnp.where(name >= 0, owner[0, jnp.maximum(name, 0)], targets)
    lhs = sides(raw[...])
    for k in range(depth):
        copies[k].wait()
        for s in range(slots):
            add_tile(lhs[k], tiles, aim, k * slots + s, total)
    lay_out(size, n_col, 0, [total], keep, send)


def add_tile(lhs, tiles, aim, i, total):
    t = aim[i]
    total[t] += jnp.dot(lhs, tiles[i], preferred_element_type=jnp.float32)


def late_kernel(size, count, *refs):
    others, (tiles, aim, send, keep, totals) = refs[:count], refs[count:]
    slots = aim.shape[0] // others[0].shape[1]
    totals[...] = jnp.zeros(totals.shape, totals.dtype)
    for h, raw in enumerate(others):
        lhs = sides(raw[...])
        for i in range(aim.shape[0]):
            add_tile(lhs[i // slots], tiles, aim, i, totals.at[h])
    lay_out(size, count + 1, 1, [totals.at[h] for h in range(count)], keep, send)


def early_sums_kernel(keep, got, ahead, out):
    sums = [keep[at] + got[at] for at in range(4)]
    encode(sums[1:3], ahead)
    out[0] = sums[0]
    out[1] = sums[3]


def side_kernel(late_keep, late_got, side):
    count = late_keep.shape[0]
    encode([late_keep[i] + late_got[i] for at in (1, 2) for i in range(at, count, 4)], side)


def near_kernel(early, late_keep, late_got, diagonal, out):
    count = late_keep.shape[0]
    encode([early[0]] + [late_keep[i] + late_got[i] for i in range(0, count, 4)], diagonal)
    out[0] = early[1]
    for h, i in enumerate(range(3, count, 4)):
        out[1 + h] = late_keep[i] + late_got[i]


def emit(groups, values, outs):
    at = 0
    for out, count in zip(outs, groups):
        if out is outs[-1]:
            for i in range(count):
                out[i] = values[at + i]
        else:
            encode(values[at : at + count], out)
        at += count


def pass_kernel(rows, each, ahead, side, out):
    late = (side.shape[0] // rows) // 2
    out[:rows, :] = ahead[rows : 2 * rows, :]
    out[rows : (1 + late) * rows, :] = side[late * rows : 2 * late * rows, :]
    first = ahead[ahead.shape[0] - SPARE :, :].astype(jnp.int32)[each : 2 * each]
    rest = side[2 * late * rows :, :].astype(jnp.int32)[late * each : 2 * late * each]
    last = out.shape[0] - (1 + late) * rows
    lines = [first, rest]
    if last > (1 + late) * each:
        lines.append(jnp.zeros((last - (1 + late) * each, LANES), jnp.int32))
    out[(1 + late) * rows :, :] = jnp.concatenate(lines, axis=0).astype(jnp.int16)


def sort_kernel(n_col, near, far, groups, keep, ahead, side, diagonal, passed, *refs):
    outs, sums = refs[:-1], refs[-1]
    rows, width = keep.shape[1:]
    for h in range(n_col):
        x = keep[h] + (decode(ahead, 0, rows, width) if h == 0 else decode(side, h - 1, rows, width))
        x = x + decode(passed, h, rows, width)
        sums[h] = x + decode(diagonal, h, rows, width)
    high, col = lax.axis_index("row") // near, lax.axis_index("col")
    emit(groups, [sums[lax.rem(col + n_col - (high ^ j), n_col)] for j in far], outs)


def far_kernel(groups, arrived, keep, *refs):
    coded, outs = refs[:arrived], refs[arrived:]
    rows, width = keep.shape[1:]
    values = []
    for i in range(sum(groups)):
        x = keep[i]
        for part in coded:
            x = x + decode(part, i, rows, width)
        values.append(x)
    emit(groups, values, outs)


def last_kernel(targets, size, keep, *refs):
    coded, out = refs[:-1], refs[-1]
    x = keep[0]
    for part in coded:
        x = x + decode(part, 0, targets * size, x.shape[1])
    for t in range(targets):
        out[:, t, :] = x[t * size : (t + 1) * size, :]


def offsets(masks):
    order = [0]
    for mask in masks:
        order = [mask | o for o in order] + order
    return order


def body(n_row, n_col, amplitudes, integrals, screen, owner_map):
    half, depth, width = amplitudes.shape
    slots, targets, out_width = integrals.shape[1], owner_map.shape[1], integrals.shape[3]
    size = half * n_col // n_row
    near = n_row // n_col
    spec = pl.BlockSpec(memory_space=pltpu.VMEM)
    smem = pl.BlockSpec(memory_space=pltpu.SMEM)
    hbm = pl.BlockSpec(memory_space=pltpu.HBM)
    params = pltpu.CompilerParams(vmem_limit_bytes=24 * 1024 * 1024)
    block = (targets * size, out_width)

    def vmem(x):
        return pltpu.with_memory_space_constraint(x, pltpu.VMEM)

    def swap(x, mask):
        return lax.ppermute(x, "row", [(i, i ^ mask) for i in range(n_row)])

    def call(kernel, name, out_shape, *operands, **more):
        single = not isinstance(out_shape, list)
        return pl.pallas_call(
            kernel,
            out_shape=out_shape,
            in_specs=[spec] * len(operands),
            out_specs=spec if single else [spec] * len(out_shape),
            compiler_params=params,
            name=name,
            **more,
        )(*[vmem(x) for x in operands])

    def coded(count, more=0):
        count *= out_width // LANES
        return pltpu.VMEM((count * block[0] + more + spare(count), LANES), jnp.int16)

    def kept(count):
        return pltpu.VMEM((count,) + block, jnp.float32)

    others = [
        lax.ppermute(amplitudes, "col", [(i, (i + step) % n_col) for i in range(n_col)])
        for step in range(1, n_col)
    ]
    half_cost = pl.CostEstimate(
        flops=2 * half * depth * targets * width * out_width, bytes_accessed=0, transcendentals=0
    )
    tiles, aim, send, keep = pl.pallas_call(
        functools.partial(early_kernel, size, n_col),
        out_shape=[
            pltpu.VMEM((depth * slots, width, out_width), jnp.bfloat16),
            pltpu.SMEM((depth * slots,), jnp.int32),
            kept(4),
            kept(4),
        ],
        in_specs=[hbm] * 4,
        out_specs=[spec, smem, spec, spec],
        scratch_shapes=[
            pltpu.SMEM(screen.shape, jnp.int32),
            pltpu.SMEM(owner_map.shape, jnp.int32),
            pltpu.VMEM(amplitudes.shape, jnp.bfloat16),
            pltpu.VMEM((targets + 1, half, out_width), jnp.float32),
            pltpu.SemaphoreType.DMA((depth,)),
            pltpu.SemaphoreType.DMA((3,)),
        ],
        cost_estimate=pl.CostEstimate(
            flops=half_cost.flops, bytes_accessed=integrals.size * 2, transcendentals=0
        ),
        compiler_params=params,
        name="early_half",
    )(*[pltpu.with_memory_space_constraint(x, pltpu.HBM) for x in (screen, owner_map, amplitudes, integrals)])
    got = swap(send, 1)

    lates = n_col - 1
    late_send, late_keep = pl.pallas_call(
        functools.partial(late_kernel, size, lates),
        out_shape=[kept(lates * 4), kept(lates * 4)],
        in_specs=[spec] * n_col + [smem],
        out_specs=[spec, spec],
        scratch_shapes=[
            pltpu.VMEM((lates, targets + 1, half, out_width), jnp.float32),
        ],
        cost_estimate=half_cost,
        compiler_params=params,
        name="late_half",
    )(*[vmem(o) for o in others], vmem(tiles), pltpu.with_memory_space_constraint(aim, pltpu.SMEM))
    late_got = swap(late_send, 1)
    def to_side(x):
        return lax.ppermute(x, "row", [(i, i ^ (ALONG if i % 2 else ACROSS) ^ 1) for i in range(n_row)])

    ahead, early = call(early_sums_kernel, "early_sums", [coded(2, SPARE), kept(2)], keep, got)
    ahead = to_side(ahead)
    side = call(side_kernel, "side_sums", coded(2 * lates), late_keep, late_got)
    diagonal, keep = call(near_kernel, "near_sums", [coded(n_col), kept(n_col)], early, late_keep, late_got)
    side = to_side(side)
    diagonal = swap(diagonal, ACROSS | ALONG | 1)
    each = out_width // LANES
    passed = call(functools.partial(pass_kernel, each * block[0], each), "pass_on", coded(n_col), ahead, side)
    arrived = [ahead, side, diagonal, swap(passed, 1)]

    masks = [near << b for b in range(n_col.bit_length() - 1)]
    plans, far = [], [0]
    for stage in reversed(pairs_of(masks)):
        partners = offsets(stage)
        plans.insert(0, (partners, len(far)))
        far = [p | o for p in partners for o in far]
    for at, (partners, count) in enumerate(plans):
        groups = [count] * len(partners)
        if at == 0:
            offs = [o // near for o in far]
            kernel = functools.partial(sort_kernel, n_col, near, offs, groups)
            more = dict(scratch_shapes=[pltpu.VMEM((n_col,) + block, jnp.float32)])
        else:
            kernel, more = functools.partial(far_kernel, groups, len(arrived)), {}
        *parts, keep = call(
            kernel, "far_sums", [coded(count)] * (len(partners) - 1) + [kept(count)], keep, *arrived, **more
        )
        arrived = [swap(part, partner | 1) for part, partner in zip(parts, partners)]
    return pl.pallas_call(
        functools.partial(last_kernel, targets, size),
        out_shape=jax.ShapeDtypeStruct((size, targets, out_width), jnp.float32),
        in_specs=[spec] * (1 + len(arrived)),
        out_specs=spec,
        compiler_params=params,
        name="own_block",
    )(vmem(keep), *[vmem(part) for part in arrived])


def solution(mesh):
    return jax.shard_map(
        functools.partial(body, mesh.shape["row"], mesh.shape["col"]),
        mesh=mesh,
        in_specs=(
            P("col", "row", None),
            P("row", "col", None, None),
            P("row", "col"),
            P("col", None),
        ),
        out_specs=P("row", "col", None),
        check_vma=False,
    )
```

```python
import functools

import jax
import jax.numpy as jnp
from jax import lax
from jax.experimental import pallas as pl
from jax.experimental.pallas import tpu as pltpu
from jax.sharding import PartitionSpec as P

SPARE = 16
LEAST = -100
LANES = 128
PARTS = (3, 4, 5, 6)
ACROSS, ALONG = 2, 4


def place(size, total, places):
    targets, near = total.shape[0] - 1, total.shape[1] // size
    low = lax.rem(lax.axis_index("row"), near)
    for ref, at, offset in places:
        first = pl.multiple_of((low ^ offset) * size, size)
        for t in range(targets):
            ref[at, t * size : (t + 1) * size, :] = total[t, pl.ds(first, size), :]


def pairs_of(masks):
    return [masks[at : at + 2] for at in range(0, len(masks), 2)]


def lay_out(size, n_col, step, totals, keep, send):
    row, col = lax.axis_index("row"), lax.axis_index("col")
    second = lax.rem(row, 2) == 1
    mine, other = jnp.where(second, ALONG, ACROSS), jnp.where(second, ACROSS, ALONG)
    near = totals[0].shape[1] // size
    for h, total in enumerate(totals):
        offset = (row // near) ^ lax.rem(col + n_col - step - h, n_col)
        flip = 0
        for stage in pairs_of([1 << b for b in range(n_col.bit_length() - 1)]):
            flip = flip ^ jnp.where(offset & sum(stage) != 0, 1, 0)
        kept = (ACROSS | ALONG | 1, mine ^ 1, mine, 0)
        sent = (ACROSS | ALONG, other, other ^ 1, 1)
        places = [(keep, 4 * h + at, j ^ flip) for at, j in enumerate(kept)]
        place(size, total, places + [(send, 4 * h + at, j ^ flip) for at, j in enumerate(sent)])


def sides(raw):
    by_tile = jnp.swapaxes(raw, 0, 1)
    return [by_tile[k] for k in range(by_tile.shape[0])]


def spare(count):
    return -(-count // SPARE) * SPARE


def encode(values, out):
    rows, width = values[0].shape
    pieces = [x[:, c : c + LANES] for x in values for c in range(0, width, LANES)]
    last = spare(len(pieces))
    at_row = lax.broadcasted_iota(jnp.int32, (last, LANES), 0)
    exponents = jnp.zeros((last, LANES), jnp.int32)
    for at, x in enumerate(pieces):
        largest = jnp.maximum(jnp.max(jnp.abs(x), axis=0, keepdims=True), 2.0**LEAST)
        exponent = jnp.floor(jnp.log2(largest)) + 1.0
        code = jnp.round(x * jnp.exp2(15.0 - exponent))
        code = jnp.clip(code, -32767.0, 32767.0).astype(jnp.int32)
        out[at * rows : (at + 1) * rows, :] = code.astype(jnp.int16)
        exponents = jnp.where(at_row == at, exponent.astype(jnp.int32), exponents)
    data = len(pieces) * rows
    for at in range(data, out.shape[0] - last, SPARE):
        out[at : at + SPARE, :] = jnp.zeros((SPARE, LANES), jnp.int16)
    out[out.shape[0] - last :, :] = exponents.astype(jnp.int16)


def decode(coded, at, rows, width):
    each = width // LANES
    count = coded.shape[0] // rows
    exponents = coded[coded.shape[0] - spare(count) :, :].astype(jnp.int32)
    parts = []
    for i in range(at * each, (at + 1) * each):
        code = coded[i * rows : (i + 1) * rows, :].astype(jnp.int32).astype(jnp.float32)
        parts.append(code * jnp.exp2(exponents[i : i + 1, :].astype(jnp.float32) - 15.0))
    return jnp.concatenate(parts, axis=1)


def list_live(screen, owner, live):
    depth, slots = screen.shape
    end = depth * slots
    for at in range(end):
        for n, value in enumerate((0, 0, owner.shape[1])):
            live[n * (end + 1) + at] = value
    count = 0
    for k in range(depth):
        for s in range(slots):
            name = screen[k, s]
            at = jnp.where(name >= 0, count, end)
            for n, value in enumerate((k * slots + s, k, owner[0, jnp.maximum(name, 0)])):
                live[n * (end + 1) + at] = value
            count = count + jnp.where(name >= 0, 1, 0)
    live[end] = count


def early_kernel(
    size, n_col, screen_hbm, owner_hbm, own_hbm, integrals,
    tiles, live, send, keep, screen, owner, aim, raw, total, sems, small,
):
    depth, slots = screen.shape
    targets = owner.shape[1]
    loads = [
        pltpu.make_async_copy(src, dst, small.at[at])
        for at, (src, dst) in enumerate(((screen_hbm, screen), (owner_hbm, owner), (own_hbm, raw)))
    ]

    for load in loads:
        load.start()
    copies = [
        pltpu.make_async_copy(integrals.at[k], tiles.at[pl.ds(k * slots, slots)], sems.at[k]) for k in range(depth)
    ]
    for at, copy in enumerate(copies):
        copy.start(priority=min(at, 1))
    total[...] = jnp.zeros(total.shape, total.dtype)
    for load in loads:
        load.wait()
    for k in range(depth):
        for s in range(slots):
            name = screen[k, s]
            aim[k * slots + s] = jnp.where(name >= 0, owner[0, jnp.maximum(name, 0)], targets)
    list_live(screen, owner, live)
    lhs = sides(raw[...])
    for k in range(depth):
        copies[k].wait()
        for s in range(slots):
            add_tile(lhs[k], tiles, aim, k * slots + s, total)
    lay_out(size, n_col, 0, [total], keep, send)


def add_tile(lhs, tiles, aim, i, total):
    t = aim[i]
    total[t] += jnp.dot(lhs, tiles[i], preferred_element_type=jnp.float32)


def late_kernel(size, count, *refs):
    others, (tiles, live, out, keep, send, lhs, totals) = refs[:count], refs[count:]
    slots = tiles.shape[0]
    totals[...] = jnp.zeros(totals.shape, totals.dtype)
    for h, raw in enumerate(others):
        for k, side in enumerate(sides(raw[...])):
            lhs[k, h] = side
    sizes = [0] + [slots * part // 6 for part in PARTS]
    for low, high in zip(sizes, sizes[1:]):

        @pl.when(jnp.logical_and(live[slots] > low, live[slots] <= high))
        def _():
            for h in range(count):
                for i in range(high):
                    tile, k, t = (live[n * (slots + 1) + i] for n in range(3))
                    totals[h, t] += jnp.dot(lhs[k, h], tiles[tile], preferred_element_type=jnp.float32)

    lay_out(size, count + 1, 1, [totals.at[h] for h in range(count)], keep, send)
    encode([send[i] for i in range(4 * count)], out)


def early_sums_kernel(keep, got, ahead, out):
    sums = [keep[at] + got[at] for at in range(4)]
    encode(sums[1:3], ahead)
    out[0] = sums[0]
    out[1] = sums[3]


def near_kernel(n_col, early, late_keep, late_got, side, diagonal, out):
    rows, width = early.shape[1:]
    sums = []
    for at in range(4):
        sums.append([late_keep[i] + decode(late_got, i, rows, width) for i in range(at, (n_col - 1) * 4, 4)])
    encode(sums[1] + sums[2], side)
    encode([early[0]] + sums[0], diagonal)
    out[0] = early[1]
    for h in range(n_col - 1):
        out[1 + h] = sums[3][h]


def emit(groups, values, outs):
    at = 0
    for out, count in zip(outs, groups):
        if out is outs[-1]:
            for i in range(count):
                out[i] = values[at + i]
        else:
            encode(values[at : at + count], out)
        at += count


def pass_kernel(rows, each, ahead, side, out):
    late = (side.shape[0] // rows) // 2
    out[:rows, :] = ahead[rows : 2 * rows, :]
    out[rows : (1 + late) * rows, :] = side[late * rows : 2 * late * rows, :]
    first = ahead[ahead.shape[0] - SPARE :, :].astype(jnp.int32)[each : 2 * each]
    rest = side[2 * late * rows :, :].astype(jnp.int32)[late * each : 2 * late * each]
    last = out.shape[0] - (1 + late) * rows
    lines = [first, rest]
    if last > (1 + late) * each:
        lines.append(jnp.zeros((last - (1 + late) * each, LANES), jnp.int32))
    out[(1 + late) * rows :, :] = jnp.concatenate(lines, axis=0).astype(jnp.int16)


def sort_kernel(n_col, near, far, groups, keep, ahead, side, diagonal, passed, *refs):
    outs, sums = refs[:-1], refs[-1]
    rows, width = keep.shape[1:]
    for h in range(n_col):
        x = keep[h] + (decode(ahead, 0, rows, width) if h == 0 else decode(side, h - 1, rows, width))
        x = x + decode(passed, h, rows, width)
        sums[h] = x + decode(diagonal, h, rows, width)
    high, col = lax.axis_index("row") // near, lax.axis_index("col")
    emit(groups, [sums[lax.rem(col + n_col - (high ^ j), n_col)] for j in far], outs)


def far_kernel(groups, arrived, keep, *refs):
    coded, outs = refs[:arrived], refs[arrived:]
    rows, width = keep.shape[1:]
    values = []
    for i in range(sum(groups)):
        x = keep[i]
        for part in coded:
            x = x + decode(part, i, rows, width)
        values.append(x)
    emit(groups, values, outs)


def last_kernel(targets, size, keep, *refs):
    coded, out = refs[:-1], refs[-1]
    x = keep[0]
    for part in coded:
        x = x + decode(part, 0, targets * size, x.shape[1])
    for t in range(targets):
        out[:, t, :] = x[t * size : (t + 1) * size, :]


def offsets(masks):
    order = [0]
    for mask in masks:
        order = [mask | o for o in order] + order
    return order


def body(n_row, n_col, amplitudes, integrals, screen, owner_map):
    half, depth, width = amplitudes.shape
    slots, targets, out_width = integrals.shape[1], owner_map.shape[1], integrals.shape[3]
    size = half * n_col // n_row
    near = n_row // n_col
    spec = pl.BlockSpec(memory_space=pltpu.VMEM)
    smem = pl.BlockSpec(memory_space=pltpu.SMEM)
    hbm = pl.BlockSpec(memory_space=pltpu.HBM)
    params = pltpu.CompilerParams(vmem_limit_bytes=24 * 1024 * 1024)
    block = (targets * size, out_width)

    def vmem(x):
        return pltpu.with_memory_space_constraint(x, pltpu.VMEM)

    def swap(x, mask):
        return lax.ppermute(x, "row", [(i, i ^ mask) for i in range(n_row)])

    def call(kernel, name, out_shape, *operands, **more):
        single = not isinstance(out_shape, list)
        return pl.pallas_call(
            kernel,
            out_shape=out_shape,
            in_specs=[spec] * len(operands),
            out_specs=spec if single else [spec] * len(out_shape),
            compiler_params=params,
            name=name,
            **more,
        )(*[vmem(x) for x in operands])

    def coded(count, more=0):
        count *= out_width // LANES
        return pltpu.VMEM((count * block[0] + more + spare(count), LANES), jnp.int16)

    def kept(count):
        return pltpu.VMEM((count,) + block, jnp.float32)

    others = [
        lax.ppermute(amplitudes, "col", [(i, (i + step) % n_col) for i in range(n_col)])
        for step in range(1, n_col)
    ]
    half_cost = pl.CostEstimate(
        flops=2 * half * depth * targets * width * out_width, bytes_accessed=0, transcendentals=0
    )
    tiles, live, send, keep = pl.pallas_call(
        functools.partial(early_kernel, size, n_col),
        out_shape=[
            pltpu.VMEM((depth * slots, width, out_width), jnp.bfloat16),
            pltpu.SMEM((3 * (depth * slots + 1),), jnp.int32),
            kept(4),
            kept(4),
        ],
        in_specs=[hbm] * 4,
        out_specs=[spec, smem, spec, spec],
        scratch_shapes=[
            pltpu.SMEM(screen.shape, jnp.int32),
            pltpu.SMEM(owner_map.shape, jnp.int32),
            pltpu.SMEM((depth * slots,), jnp.int32),
            pltpu.VMEM(amplitudes.shape, jnp.bfloat16),
            pltpu.VMEM((targets + 1, half, out_width), jnp.float32),
            pltpu.SemaphoreType.DMA((depth,)),
            pltpu.SemaphoreType.DMA((3,)),
        ],
        cost_estimate=pl.CostEstimate(
            flops=half_cost.flops, bytes_accessed=integrals.size * 2, transcendentals=0
        ),
        compiler_params=params,
        name="early_half",
    )(*[pltpu.with_memory_space_constraint(x, pltpu.HBM) for x in (screen, owner_map, amplitudes, integrals)])
    got = swap(send, 1)

    lates = n_col - 1
    late_send, late_keep = pl.pallas_call(
        functools.partial(late_kernel, size, lates),
        out_shape=[coded(lates * 4), kept(lates * 4)],
        in_specs=[spec] * n_col + [smem],
        out_specs=[spec, spec],
        scratch_shapes=[
            pltpu.VMEM((lates * 4,) + block, jnp.float32),
            pltpu.VMEM((depth, lates, half, width), jnp.bfloat16),
            pltpu.VMEM((lates, targets + 1, half, out_width), jnp.float32),
        ],
        cost_estimate=half_cost,
        compiler_params=params,
        name="late_half",
    )(*[vmem(o) for o in others], vmem(tiles), pltpu.with_memory_space_constraint(live, pltpu.SMEM))
    late_got = swap(late_send, 1)
    def to_side(x):
        return lax.ppermute(x, "row", [(i, i ^ (ALONG if i % 2 else ACROSS) ^ 1) for i in range(n_row)])

    ahead, early = call(early_sums_kernel, "early_sums", [coded(2, SPARE), kept(2)], keep, got)
    ahead = to_side(ahead)
    side, diagonal, keep = call(
        functools.partial(near_kernel, n_col),
        "near_sums",
        [coded(2 * lates), coded(n_col), kept(n_col)],
        early,
        late_keep,
        late_got,
    )
    side = to_side(side)
    diagonal = swap(diagonal, ACROSS | ALONG | 1)
    each = out_width // LANES
    passed = call(functools.partial(pass_kernel, each * block[0], each), "pass_on", coded(n_col), ahead, side)
    arrived = [ahead, side, diagonal, swap(passed, 1)]

    masks = [near << b for b in range(n_col.bit_length() - 1)]
    plans, far = [], [0]
    for stage in reversed(pairs_of(masks)):
        partners = offsets(stage)
        plans.insert(0, (partners, len(far)))
        far = [p | o for p in partners for o in far]
    for at, (partners, count) in enumerate(plans):
        groups = [count] * len(partners)
        if at == 0:
            offs = [o // near for o in far]
            kernel = functools.partial(sort_kernel, n_col, near, offs, groups)
            more = dict(scratch_shapes=[pltpu.VMEM((n_col,) + block, jnp.float32)])
        else:
            kernel, more = functools.partial(far_kernel, groups, len(arrived)), {}
        *parts, keep = call(
            kernel, "far_sums", [coded(count)] * (len(partners) - 1) + [kept(count)], keep, *arrived, **more
        )
        arrived = [swap(part, partner | 1) for part, partner in zip(parts, partners)]
    return pl.pallas_call(
        functools.partial(last_kernel, targets, size),
        out_shape=jax.ShapeDtypeStruct((size, targets, out_width), jnp.float32),
        in_specs=[spec] * (1 + len(arrived)),
        out_specs=spec,
        compiler_params=params,
        name="own_block",
    )(vmem(keep), *[vmem(part) for part in arrived])


def solution(mesh):
    return jax.shard_map(
        functools.partial(body, mesh.shape["row"], mesh.shape["col"]),
        mesh=mesh,
        in_specs=(
            P("col", "row", None),
            P("row", "col", None, None),
            P("row", "col"),
            P("col", None),
        ),
        out_specs=P("row", "col", None),
        check_vma=False,
    )
```
